128 devices in a mesh: dp: 16 (over z, y), ctx: 8 (over x, core).
Axes of the slice: x: 4, y: 4, z: 4, core: 2. Of those that a mesh axis runs over, the one named last changes fastest.
Arguments:
- queries: bfloat16 [16384, 4096], P(('dp', 'ctx')), may hold values from -40 to 40
- loader_key_rows: bfloat16 [16384, 512], P(('dp', 'ctx')), may hold values from -40 to 40
- loader_value_rows: bfloat16 [16384, 512], P(('dp', 'ctx')), may hold values from -6 to 6
- output_gradient: bfloat16 [16384, 4096], P(('dp', 'ctx')), may hold values from -6 to 6
- packing: int32 [128, 128], P(('dp', 'ctx')), may hold values from 0 to 127, each once within a row
- documents: int32 [16, 1024], P('dp'), may hold values from 0 to 3, never falling along the last dimension, each value on 1 to 512 neighbouring positions
Outputs:
- attn_out: bfloat16 [16384, 4096], P(('dp', 'ctx'))
- grad_queries: float32 [16384, 4096], P(('dp', 'ctx'))
- key_gradients: float32 [16384, 512], P(('dp', 'ctx'))
- value_gradients: float32 [16384, 512], P(('dp', 'ctx'))
The draws below stay inside these ranges and needn't reach their ends.
Inputs may be any that keep to these rules, and one draw needn't show every extreme that they name: `packing`: each row holds every number of 0 to 127 once. `documents`: ids never fall along a sequence; each document has 1 to 512 positions, one exactly 512.
All inputs are finite; a program needn't handle non-finite values.
Results may differ from the reference program's by a relative error of at most 0.04.
Values may be sent and summed in bfloat16 or wider, within the bound.
A program may use at most 64 MiB of HBM per device.

```python
import math
import jax
import jax.numpy as jnp
import numpy as np
from jax import lax

QUERY_HEADS = 32
KEY_HEADS = 4
HEAD_WIDTH = 128
TOK_DEV = 128
DOCS = 4
QUERY_PER_KEY = 8
SEQUENCE_LENGTH = 1024
TOKEN_ROWS = 16384
DOC_MOST = 512
N_DP = 16
N_CTX = 8


def draw_loader_key_rows(key, part):
    key = jax.random.fold_in(key, 11)
    random_noise = jax.random.normal(key, (TOKEN_ROWS, KEY_HEADS, HEAD_WIDTH), jnp.float32)
    value_matrix = random_noise
    return jnp.clip(value_matrix, -40.0, 40.0).reshape(TOKEN_ROWS, KEY_HEADS * HEAD_WIDTH).astype(jnp.bfloat16)


def draw_queries(key, part):
    key = jax.random.fold_in(key, 12)
    random_noise_key = jax.random.fold_in(key, 0)
    random_noise = jax.random.normal(random_noise_key, (TOKEN_ROWS, KEY_HEADS, QUERY_PER_KEY, HEAD_WIDTH), jnp.float32)
    value_matrix = random_noise
    return jnp.clip(value_matrix, -40.0, 40.0).reshape(TOKEN_ROWS, QUERY_HEADS * HEAD_WIDTH).astype(jnp.bfloat16)


def block_levels(stream_key, shape, cuts, smallest, high):
    def one(axis_at, blocks):
        steps = jax.random.uniform(jax.random.fold_in(jax.random.fold_in(stream_key, 6), axis_at), (blocks,), jnp.float32, smallest / len(cuts), high / len(cuts))
        return jnp.repeat(jnp.exp(steps), shape[axis_at] // blocks).reshape((-1,) + (1,) * (len(shape) - axis_at - 1))

    factor_of = one(*cuts[0])
    for cut in cuts[1:]:
        factor_of = factor_of * one(*cut)
    return factor_of


def split_up(number_of, total, limit, lean):
    weights = [(1 << 20) // math.isqrt(grade ** lean) + 1 for grade in range(2, number_of + 1)]
    rest, holding = total - limit - (number_of - 1), [1] * (number_of - 1)
    while rest > 0:
        movable = [i for i in range(number_of - 1) if holding[i] < limit]
        pool, budget = sum([weights[i] for i in movable]), rest
        for i in movable:
            extra = min(limit - holding[i], max(1, budget * weights[i] // pool), rest)
            holding[i] = holding[i] + extra
            rest = rest - extra
    return np.array([limit] + holding)


def uneven_parts(key, count, total, bound, skew):
    if count == 2:
        one = jax.random.randint(key, (), max(1, total - bound), min(bound, total - 1) + 1)
        return jnp.stack([one, total - one])
    tallies = jnp.asarray(split_up(count, total, bound, skew), jnp.int32)
    pairs = (count - 1) // 2
    donor, receiver = tallies[1:1 + 2 * pairs:2], tallies[2:2 + 2 * pairs:2]
    slack = jnp.minimum(donor - 1, bound - receiver)
    moved = jax.random.randint(jax.random.fold_in(key, 1), (pairs,), 0, 1 << 20) % (slack + 1)
    tallies = tallies.at[1:1 + 2 * pairs:2].set(donor - moved).at[2:2 + 2 * pairs:2].set(receiver + moved)
    return tallies[jax.random.permutation(jax.random.fold_in(key, 2), count)]


def noise(own_key, extent, width, limit, cuts=(), held_as=jnp.bfloat16):
    gain = block_levels(own_key, extent, cuts, -0.22, 0.18) if cuts else 1.0
    values = jax.random.normal(own_key, extent, jnp.float32) * width * gain
    return jnp.minimum(jnp.maximum(values, -limit), limit).astype(held_as)


def setup_inputs(seed: int = 0) -> dict:
    keys = jax.random.split(jax.random.key(seed), 7)
    return {
        "queries": draw_queries(jax.random.fold_in(keys[6], 71), 0),
        "loader_key_rows": draw_loader_key_rows(jax.random.fold_in(keys[6], 71), 0),
        "loader_value_rows": noise(keys[2], (TOKEN_ROWS, KEY_HEADS * HEAD_WIDTH), 1.0, 6.0, ((0, 128),)),
        "output_gradient": noise(keys[3], (TOKEN_ROWS, QUERY_HEADS * HEAD_WIDTH), 1.0, 6.0, ((0, 128),)),
        "packing": jax.vmap(lambda own: jax.random.permutation(own, TOK_DEV))(jax.random.split(keys[4], (N_DP * N_CTX))).reshape((N_DP * N_CTX, TOK_DEV)).astype(jnp.int32),
        "documents": jax.vmap(lambda own: jnp.searchsorted(jnp.cumsum(uneven_parts(own, DOCS, SEQUENCE_LENGTH, DOC_MOST, 2)), jnp.arange(SEQUENCE_LENGTH), side="right"))(jax.random.split(keys[5], N_DP)).reshape((N_DP, SEQUENCE_LENGTH)).astype(jnp.int32),
    }


def group_attention(operands):
    query_g, key_g, value_g, grad_g, causal_mask = operands
    scale = 1.0 / math.sqrt(HEAD_WIDTH)
    scores = jnp.einsum('qrd,kd->rqk', query_g.astype(jnp.float32), key_g.astype(jnp.float32)) * scale
    masked = jnp.where(causal_mask[None], scores, -1e+30)
    best = lax.optimization_barrier(jnp.max(masked, axis=-1, keepdims=True))
    total = lax.optimization_barrier(jnp.sum(jnp.where(causal_mask[None], jnp.exp(masked - best), 0.0), axis=-1, keepdims=True))
    log_sum = best + jnp.log(total)
    probs = jnp.where(causal_mask[None], jnp.exp(scores - log_sum), 0.0)
    probs_b = probs.astype(jnp.bfloat16)
    attention_output = jnp.einsum('rqk,kd->qrd', probs_b.astype(jnp.float32), value_g.astype(jnp.float32)).astype(jnp.bfloat16)
    delta = lax.optimization_barrier(jnp.sum(attention_output.astype(jnp.float32) * grad_g.astype(jnp.float32), axis=-1)).T
    dprob = jnp.einsum('qrd,kd->rqk', grad_g.astype(jnp.float32), value_g.astype(jnp.float32))
    dscore = (probs * (dprob - delta[:, :, None]) * scale).astype(jnp.bfloat16)
    query_gradient = jnp.einsum('rqk,kd->qrd', dscore.astype(jnp.float32), key_g.astype(jnp.float32))
    key_gradient = jnp.einsum('rqk,qrd->kd', dscore.astype(jnp.float32), query_g.astype(jnp.float32))
    value_gradient = jnp.einsum('rqk,qrd->kd', probs_b.astype(jnp.float32), grad_g.astype(jnp.float32))
    return (attention_output, query_gradient, key_gradient, value_gradient)

def reference(queries, loader_key_rows, loader_value_rows, output_gradient, packing, documents):
    devices = N_DP * N_CTX
    slot_rows = TOK_DEV // devices
    position = jnp.arange(SEQUENCE_LENGTH, dtype=jnp.int32)
    within = position % TOK_DEV
    source = (within // slot_rows).astype(jnp.int32)
    sequence = jnp.arange(N_DP, dtype=jnp.int32)[:, None]
    column = (sequence * N_CTX + (position // TOK_DEV)[None, :]) * slot_rows + (within % slot_rows)[None, :]
    packed = (source[None, :] * TOK_DEV + packing[source[None, :], column]).astype(jnp.int32)

    def one_sequence(operands):
        row_identifiers, doc_line = operands
        causal_mask = (position[None, :] <= position[:, None]) & (doc_line[None, :] == doc_line[:, None])
        sliced_queries = queries[row_identifiers].reshape(SEQUENCE_LENGTH, KEY_HEADS, QUERY_PER_KEY, HEAD_WIDTH).transpose(1, 0, 2, 3)
        score_gradient = output_gradient[row_identifiers].reshape(SEQUENCE_LENGTH, KEY_HEADS, QUERY_PER_KEY, HEAD_WIDTH).transpose(1, 0, 2, 3)
        sliced_keys = loader_key_rows[row_identifiers].reshape(SEQUENCE_LENGTH, KEY_HEADS, HEAD_WIDTH).transpose(1, 0, 2)
        sliced_values = loader_value_rows[row_identifiers].reshape(SEQUENCE_LENGTH, KEY_HEADS, HEAD_WIDTH).transpose(1, 0, 2)
        document_masks = jnp.broadcast_to(causal_mask[None], (KEY_HEADS, SEQUENCE_LENGTH, SEQUENCE_LENGTH))
        attention_output, query_gradient, key_gradient, value_gradient = lax.map(group_attention, (sliced_queries, sliced_keys, sliced_values, score_gradient, document_masks))
        return (attention_output.transpose(1, 0, 2, 3).reshape(SEQUENCE_LENGTH, QUERY_HEADS * HEAD_WIDTH), query_gradient.transpose(1, 0, 2, 3).reshape(SEQUENCE_LENGTH, QUERY_HEADS * HEAD_WIDTH), key_gradient.transpose(1, 0, 2).reshape(SEQUENCE_LENGTH, KEY_HEADS * HEAD_WIDTH), value_gradient.transpose(1, 0, 2).reshape(SEQUENCE_LENGTH, KEY_HEADS * HEAD_WIDTH))
    attention_output, query_gradient, key_gradient, value_gradient = lax.map(one_sequence, (packed, documents))
    flattened = packed.reshape(-1)
    attn_out = jnp.zeros(queries.shape, queries.dtype).at[flattened].set(attention_output.reshape(TOKEN_ROWS, QUERY_HEADS * HEAD_WIDTH))
    grad_queries = jnp.zeros(queries.shape, jnp.float32).at[flattened].set(query_gradient.reshape(TOKEN_ROWS, QUERY_HEADS * HEAD_WIDTH))
    key_gradients = jnp.zeros(loader_key_rows.shape, jnp.float32).at[flattened].set(key_gradient.reshape(TOKEN_ROWS, KEY_HEADS * HEAD_WIDTH))
    value_gradients = jnp.zeros(loader_value_rows.shape, jnp.float32).at[flattened].set(value_gradient.reshape(TOKEN_ROWS, KEY_HEADS * HEAD_WIDTH))
    return (attn_out, grad_queries, key_gradients, value_gradients)
```

```python
import math

import jax
import jax.numpy as jnp
from jax import lax
from jax.experimental import pallas as pl
from jax.experimental.pallas import tpu as pltpu
from jax.sharding import PartitionSpec as P

HEAD_WIDTH = 128
TOK_DEV = 128
N_DP = 16
N_CTX = 8
DEVICES = N_DP * N_CTX
HEADS = 4
KEY_HEADS = 4
BLOCKS = 8
SEQ = 1024
QB = 256
DOC_MOST = 512
SCALE = 1.0 / math.sqrt(HEAD_WIDTH)
MESH = pl.DeviceIdType.MESH
F32 = jnp.float32
BF16 = jnp.bfloat16
STRIDE = 37

WINDOWS = [(max(0, QB * i - DOC_MOST), QB * (i + 1)) for i in range(SEQ // QB)]
BIAS_ROWS = [sum(b - a for a, b in WINDOWS[:i]) for i in range(len(WINDOWS) + 1)]


def shifted(device, offset):
    low = 0b0101010
    return (((device & low) + (offset & low)) ^ ((device ^ offset) & (127 - low))) & 127


def dot_nt(a, b):
    return lax.dot_general(a, b, (((1,), (1,)), ((), ())), preferred_element_type=F32)


def dot_nn(a, b):
    return jnp.dot(a, b, preferred_element_type=F32)


def wait_bytes(ref, sem):
    pltpu.make_async_copy(ref, ref, sem).wait()


def main_kernel(
    q_hbm, k_hbm, v_hbm, d_hbm, pack_hbm, docs_hbm,
    ret, retkv,
    q_in, k_in, v_in, d_in, pack, docs,
    send, recv, outb, kvsend, kvrecv, kvout, xbuf,
    scr, scr2, qs, ds, dts, ks, vs, kts, vts, dks, dvs, bias,
    load_sem, in_send, in_recv, out_send, out_recv,
    kvs_sem, kvr_sem, kvx_sem, ks_sem, kr_sem, dx_sem,
):
    my_dp = lax.axis_index("dp")
    my_ctx = lax.axis_index("ctx")
    me = my_dp * N_CTX + my_ctx
    core = my_ctx % 2
    my_key = my_ctx // 2
    half = me // 64
    sibling = {"dp": my_dp, "ctx": my_ctx + 1 - 2 * core}

    def at(device):
        return {"dp": device // N_CTX, "ctx": device % N_CTX}

    barrier = pltpu.get_barrier_semaphore()

    def greet(i, carry):
        pl.semaphore_signal(barrier, inc=1, device_id=at(shifted(me, (i * STRIDE) & 127)), device_id_type=MESH)
        return carry

    lax.fori_loop(1, DEVICES, greet, 0)

    loads = [
        pltpu.make_async_copy(src, dst, load_sem.at[i])
        for i, (src, dst) in enumerate(
            ((pack_hbm, pack), (k_hbm, k_in), (v_hbm, v_in), (q_hbm, q_in), (d_hbm, d_in), (docs_hbm, docs))
        )
    ]
    for load in loads:
        load.start()

    loads[0].wait()
    row = lax.broadcasted_iota(jnp.int32, (TOK_DEV, DEVICES), 0)
    picks = jnp.transpose(jnp.where(row == pack[...], 1.0, 0.0).astype(F32)).astype(BF16)

    def pair_rows(a, b):
        a = a.reshape(N_DP, BLOCKS, HEAD_WIDTH)
        b = b.reshape(N_DP, BLOCKS, HEAD_WIDTH)
        return jnp.concatenate([a, b], axis=1).astype(BF16)

    loads[1].wait()
    loads[2].wait()
    for j in range(KEY_HEADS):
        cols = slice(j * HEAD_WIDTH, (j + 1) * HEAD_WIDTH)
        kvsend[j] = pair_rows(dot_nn(picks, k_in[:, cols]), dot_nn(picks, v_in[:, cols]))
    loads[3].wait()
    loads[4].wait()

    def pack_head(h):
        for c in range(N_CTX):
            cols = pl.ds(pl.multiple_of((c * HEADS + h) * HEAD_WIDTH, HEAD_WIDTH), HEAD_WIDTH)
            send[h, c * N_DP : (c + 1) * N_DP] = pair_rows(dot_nn(picks, q_in[:, cols]), dot_nn(picks, d_in[:, cols]))

    pack_head(0)
    pl.semaphore_wait(barrier, DEVICES - 1)

    def send_kv_to(chip_offset):
        target = shifted(me - core, 2 * chip_offset) + half
        s, c = target // N_CTX, target % N_CTX
        return pltpu.make_async_remote_copy(
            src_ref=kvsend.at[c // 2, s], dst_ref=kvrecv.at[me], send_sem=kvs_sem, recv_sem=kvr_sem,
            device_id={"dp": s, "ctx": c}, device_id_type=MESH,
        )

    def send_kv(i, carry):
        send_kv_to((i * STRIDE) & 63).start()
        return carry

    @pl.when(core == half)
    def _():
        pltpu.make_async_copy(kvsend.at[my_key, my_dp], kvrecv.at[me], kvr_sem).start()

    @pl.when(core != half)
    def _():
        send_kv_to(0).start()

    lax.fori_loop(1, 64, send_kv, 0)

    def send_head(h):
        def step(i, carry):
            target = shifted(me, (i * STRIDE) & 127)
            s, c = target // N_CTX, target % N_CTX
            pltpu.make_async_remote_copy(
                src_ref=send.at[h, c * N_DP + s], dst_ref=recv.at[h, me], send_sem=in_send.at[h], recv_sem=in_recv.at[h],
                device_id={"dp": s, "ctx": c}, device_id_type=MESH,
            ).start()
            return carry

        pltpu.make_async_copy(send.at[h, my_ctx * N_DP + my_dp], recv.at[h, me], in_recv.at[h]).start()
        lax.fori_loop(1, DEVICES, step, 0)

    send_head(0)

    def pack_and_send(h, carry):
        pack_head(h)
        send_head(h)
        return carry

    lax.fori_loop(1, HEADS, pack_and_send, 0)

    loads[5].wait()
    doc_line = docs[...].astype(F32)
    for k in range(BLOCKS):
        block = jnp.broadcast_to(doc_line[:, k * 128 : (k + 1) * 128], (128, 128))
        scr[k * 128 : (k + 1) * 128] = jnp.transpose(block)
    for i, (lo, hi) in enumerate(WINDOWS):
        for t in range(lo, hi, 128):
            key_doc = scr[t : t + 128]
            for n in range(QB // 128):
                q0 = i * QB + n * 128
                query_doc = doc_line[:, q0 : q0 + 128]
                tpos = t + lax.broadcasted_iota(jnp.int32, (128, 128), 0)
                qpos = q0 + lax.broadcasted_iota(jnp.int32, (128, 128), 1)
                live = (key_doc == query_doc) & (tpos <= qpos)
                at_row = BIAS_ROWS[i] + t - lo
                bias[at_row : at_row + 128, n * 128 : (n + 1) * 128] = jnp.where(live, 0.0, -1e30)
    dks[...] = jnp.zeros_like(dks)
    dvs[...] = jnp.zeros_like(dvs)

    wait_bytes(kvrecv.at[pl.ds(0, 64)], kvr_sem)
    mine = kvrecv.at[pl.ds(core * 64, 64)]
    swap = pltpu.make_async_remote_copy(
        src_ref=mine, dst_ref=mine, send_sem=kvx_sem.at[0], recv_sem=kvx_sem.at[1], device_id=sibling, device_id_type=MESH
    )
    swap.start()
    swap.wait()
    scr[...] = kvrecv[...].reshape(2 * SEQ, HEAD_WIDTH).astype(F32)
    for k in range(BLOCKS):
        rows = slice(k * 128, (k + 1) * 128)
        k_block = scr[pl.ds(k, 128, stride=16), :]
        v_block = scr[pl.ds(BLOCKS + k, 128, stride=16), :]
        ks[rows] = k_block.astype(BF16)
        vs[rows] = v_block.astype(BF16)
        kts[:, rows] = jnp.transpose(k_block).astype(BF16)
        vts[:, rows] = jnp.transpose(v_block).astype(BF16)

    def one_head(h, carry):
        wait_bytes(recv.at[h], in_recv.at[h])
        scr[...] = recv[h].reshape(2 * SEQ, HEAD_WIDTH).astype(F32)
        for k in range(BLOCKS):
            rows = slice(k * 128, (k + 1) * 128)
            qs[rows] = scr[pl.ds(k, 128, stride=16), :].astype(BF16)
            d_block = scr[pl.ds(BLOCKS + k, 128, stride=16), :]
            ds[rows] = d_block.astype(BF16)
            dts[:, rows] = jnp.transpose(d_block)
        for i, (lo, hi) in enumerate(WINDOWS):
            q_rows = slice(i * QB, (i + 1) * QB)
            query, cotangent = qs[q_rows], ds[q_rows]
            scores = dot_nt(ks[lo:hi], query) + bias[BIAS_ROWS[i] : BIAS_ROWS[i + 1]]
            best = jnp.max(scores, axis=0, keepdims=True)
            weights = jnp.exp2((scores - best) * (SCALE * math.log2(math.e)))
            total = jnp.sum(weights, axis=0, keepdims=True)
            probs = weights * (1.0 / total)
            probs_b = probs.astype(BF16)
            out_t = dot_nn(vts[:, lo:hi], probs_b)
            delta = jnp.sum(out_t.astype(BF16).astype(F32) * dts[:, q_rows], axis=0, keepdims=True)
            dprob = dot_nt(vs[lo:hi], cotangent)
            dscore = (probs * (dprob - delta) * SCALE).astype(BF16)
            gq_t = dot_nn(kts[:, lo:hi], dscore)
            dks[lo:hi] += dot_nn(dscore, query)
            dvs[lo:hi] += dot_nn(probs_b, cotangent)
            for n in range(QB // 128):
                k = i * (QB // 128) + n
                lanes = slice(n * 128, (n + 1) * 128)
                scr2[pl.ds(k, 128, stride=16), :] = jnp.transpose(out_t[:, lanes])
                scr2[pl.ds(BLOCKS + k, 128, stride=16), :] = jnp.transpose(gq_t[:, lanes])
        outb[h] = scr2[...].astype(BF16).reshape(DEVICES, 16, HEAD_WIDTH)

        def step(n, inner):
            target = shifted(me, (n * STRIDE) & 127)
            pltpu.make_async_remote_copy(
                src_ref=outb.at[h, target], dst_ref=ret.at[h, my_ctx, my_dp], send_sem=out_send.at[h],
                recv_sem=out_recv.at[h], device_id=at(target), device_id_type=MESH,
            ).start()
            return inner

        pltpu.make_async_copy(outb.at[h, me], ret.at[h, my_ctx, my_dp], out_recv.at[h]).start()
        lax.fori_loop(1, DEVICES, step, 0)
        return carry

    lax.fori_loop(0, HEADS, one_head, 0)

    for k in range(BLOCKS):
        rows = slice(k * 128, (k + 1) * 128)
        scr[pl.ds(k, 128, stride=16), :] = dks[rows]
        scr[pl.ds(BLOCKS + k, 128, stride=16), :] = dvs[rows]
    swap_back = pltpu.make_async_remote_copy(
        src_ref=scr.at[pl.ds(pl.multiple_of((1 - core) * SEQ, SEQ), SEQ)], dst_ref=xbuf, send_sem=dx_sem.at[0], recv_sem=dx_sem.at[1],
        device_id=sibling, device_id_type=MESH,
    )
    swap_back.start()
    swap_back.wait()
    own_half = scr[pl.ds(pl.multiple_of(core * SEQ, SEQ), SEQ), :]
    kvout[...] = (own_half + xbuf[...]).astype(BF16).reshape(64, 16, HEAD_WIDTH)

    def return_kv_to(offset):
        slot = shifted(me, offset) & 63
        return pltpu.make_async_remote_copy(
            src_ref=kvout.at[slot], dst_ref=retkv.at[my_key, my_dp], send_sem=ks_sem, recv_sem=kr_sem,
            device_id=at(core * 64 + slot), device_id_type=MESH,
        )

    def return_kv(i, carry):
        return_kv_to((i * STRIDE) & 63).start()
        return carry

    @pl.when(core == half)
    def _():
        pltpu.make_async_copy(kvout.at[me - half * 64], retkv.at[my_key, my_dp], kr_sem).start()

    @pl.when(core != half)
    def _():
        return_kv_to(0).start()

    lax.fori_loop(1, 64, return_kv, 0)

    for h in range(HEADS):
        wait_bytes(ret.at[h], out_recv.at[h])
    wait_bytes(retkv, kr_sem)
    for h in range(HEADS):
        wait_bytes(send.at[h, pl.ds(0, DEVICES - 1)], in_send.at[h])
        wait_bytes(outb.at[h, pl.ds(0, DEVICES - 1)], out_send.at[h])

    @pl.when(core == half)
    def _():
        wait_bytes(kvrecv.at[pl.ds(0, 63)], kvs_sem)
        wait_bytes(kvout.at[pl.ds(0, 63)], ks_sem)

    @pl.when(core != half)
    def _():
        wait_bytes(kvrecv.at[pl.ds(0, 64)], kvs_sem)
        wait_bytes(kvout.at[pl.ds(0, 64)], ks_sem)


def unpack_kernel(pack, ret, retkv, out, gq, gk, gv):
    row = lax.broadcasted_iota(jnp.int32, (TOK_DEV, DEVICES), 0)
    picks = jnp.where(row == pack[...], 1.0, 0.0).astype(BF16)
    device = lax.broadcasted_iota(jnp.int32, (DEVICES, 2 * DEVICES), 0)
    lane = lax.broadcasted_iota(jnp.int32, (DEVICES, 2 * DEVICES), 1)
    same = device == (lane >> 4) * BLOCKS + (lane & 7)
    upper = ((lane >> 3) & 1) == 1
    spread = [jnp.where(same & (upper == bool(t)), 1.0, 0.0).astype(BF16) for t in range(2)]
    place = jnp.concatenate([dot_nn(picks, e) for e in spread], axis=0).astype(BF16)

    for h in range(HEADS):
        cols = slice(h * HEAD_WIDTH, (h + 1) * HEAD_WIDTH)
        both = dot_nn(place, ret[h, 0].reshape(2 * DEVICES, HEAD_WIDTH))
        out[:, cols] = both[:TOK_DEV].astype(BF16)
        gq[:, cols] = both[TOK_DEV:]

    @pl.when(pl.program_id(0) == 0)
    def _():
        for j in range(KEY_HEADS):
            cols = slice(j * HEAD_WIDTH, (j + 1) * HEAD_WIDTH)
            both = dot_nn(place, retkv[j].reshape(2 * DEVICES, HEAD_WIDTH))
            gk[:, cols] = both[:TOK_DEV]
            gv[:, cols] = both[TOK_DEV:]


def local(queries, loader_key_rows, loader_value_rows, output_gradient, packing, documents):
    slots = (DEVICES, 16, HEAD_WIDTH)
    ret, retkv = pl.pallas_call(
        main_kernel,
        out_shape=(
            jax.ShapeDtypeStruct((HEADS, N_CTX, N_DP, 16, HEAD_WIDTH), BF16),
            jax.ShapeDtypeStruct((KEY_HEADS, N_DP, 16, HEAD_WIDTH), BF16),
        ),
        in_specs=[pl.BlockSpec(memory_space=pl.ANY)] * 6,
        out_specs=(pl.BlockSpec(memory_space=pl.ANY),) * 2,
        scratch_shapes=[
            pltpu.VMEM(queries.shape, BF16),
            pltpu.VMEM(loader_key_rows.shape, BF16),
            pltpu.VMEM(loader_value_rows.shape, BF16),
            pltpu.VMEM(output_gradient.shape, BF16),
            pltpu.VMEM(packing.shape, jnp.int32),
            pltpu.VMEM(documents.shape, jnp.int32),
            pltpu.VMEM((HEADS, *slots), BF16),
            pltpu.VMEM((HEADS, *slots), BF16),
            pltpu.VMEM((HEADS, *slots), BF16),
            pltpu.VMEM((KEY_HEADS, N_DP, 16, HEAD_WIDTH), BF16),
            pltpu.VMEM(slots, BF16),
            pltpu.VMEM((64, 16, HEAD_WIDTH), BF16),
            pltpu.VMEM((SEQ, HEAD_WIDTH), F32),
            pltpu.VMEM((2 * SEQ, HEAD_WIDTH), F32),
            pltpu.VMEM((2 * SEQ, HEAD_WIDTH), F32),
            pltpu.VMEM((SEQ, HEAD_WIDTH), BF16),
            pltpu.VMEM((SEQ, HEAD_WIDTH), BF16),
            pltpu.VMEM((HEAD_WIDTH, SEQ), F32),
            pltpu.VMEM((SEQ, HEAD_WIDTH), BF16),
            pltpu.VMEM((SEQ, HEAD_WIDTH), BF16),
            pltpu.VMEM((HEAD_WIDTH, SEQ), BF16),
            pltpu.VMEM((HEAD_WIDTH, SEQ), BF16),
            pltpu.VMEM((SEQ, HEAD_WIDTH), F32),
            pltpu.VMEM((SEQ, HEAD_WIDTH), F32),
            pltpu.VMEM((BIAS_ROWS[-1], QB), F32),
            pltpu.SemaphoreType.DMA((6,)),
            pltpu.SemaphoreType.DMA((HEADS,)),
            pltpu.SemaphoreType.DMA((HEADS,)),
            pltpu.SemaphoreType.DMA((HEADS,)),
            pltpu.SemaphoreType.DMA((HEADS,)),
            pltpu.SemaphoreType.DMA,
            pltpu.SemaphoreType.DMA,
            pltpu.SemaphoreType.DMA((2,)),
            pltpu.SemaphoreType.DMA,
            pltpu.SemaphoreType.DMA,
            pltpu.SemaphoreType.DMA((2,)),
        ],
        compiler_params=pltpu.CompilerParams(collective_id=0, has_side_effects=True, vmem_limit_bytes=48 << 20),
        name="exchange_attention",
    )(queries, loader_key_rows, loader_value_rows, output_gradient, packing, documents)

    wide = HEADS * HEAD_WIDTH
    kv_shape = (TOK_DEV, KEY_HEADS * HEAD_WIDTH)
    return pl.pallas_call(
        unpack_kernel,
        grid=(N_CTX,),
        out_shape=(
            jax.ShapeDtypeStruct(queries.shape, BF16),
            jax.ShapeDtypeStruct(queries.shape, F32),
            jax.ShapeDtypeStruct(kv_shape, F32),
            jax.ShapeDtypeStruct(kv_shape, F32),
        ),
        in_specs=[
            pl.BlockSpec((1, TOK_DEV), lambda c: (0, 0)),
            pl.BlockSpec((HEADS, 1, N_DP, 16, HEAD_WIDTH), lambda c: (0, c, 0, 0, 0)),
            pl.BlockSpec((KEY_HEADS, N_DP, 16, HEAD_WIDTH), lambda c: (0, 0, 0, 0)),
        ],
        out_specs=(
            pl.BlockSpec((TOK_DEV, wide), lambda c: (0, c)),
            pl.BlockSpec((TOK_DEV, wide), lambda c: (0, c)),
            pl.BlockSpec(kv_shape, lambda c: (0, 0)),
            pl.BlockSpec(kv_shape, lambda c: (0, 0)),
        ),
        name="rows_to_loader_order",
    )(packing, ret, retkv)


def solution(mesh):
    rows = P(("dp", "ctx"), None)
    return jax.shard_map(
        local, mesh=mesh, in_specs=(rows,) * 5 + (P("dp", None),), out_specs=(rows,) * 4, check_vma=False
    )
```

```python
import math

import jax
import jax.numpy as jnp
from jax import lax
from jax.experimental import pallas as pl
from jax.experimental.pallas import tpu as pltpu
from jax.sharding import PartitionSpec as P

HEAD_WIDTH = 128
TOK_DEV = 128
N_CTX = 8
DEVICES = 128
SEQUENCES = 16
KEY_HEADS = 4
BLOCKS = 8
SEQ = 1024
QB = 256
DOC_MOST = 512
SCALE = 1.0 / math.sqrt(HEAD_WIDTH)
MESH = pl.DeviceIdType.MESH
F32 = jnp.float32
BF16 = jnp.bfloat16

Z, Y, X = range(3)
UNITS = KEY_HEADS
OWN = 2
CHUNKS = 2
CHUNK_HEADS = 4
PLANE = 32
ROWS = CHUNK_HEADS * 16
STRIDE = 13

WINDOWS = [(max(0, QB * i - DOC_MOST), QB * (i + 1)) for i in range(SEQ // QB)]
BIAS_ROWS = [sum(b - a for a, b in WINDOWS[:i]) for i in range(len(WINDOWS) + 1)]


def shifted(index, offset):
    low = 0b01010
    return (((index & low) + (offset & low)) ^ ((index ^ offset) & (31 - low))) & 31


def dot_nt(a, b):
    return lax.dot_general(a, b, (((1,), (1,)), ((), ())), preferred_element_type=F32)


def dot_nn(a, b):
    return jnp.dot(a, b, preferred_element_type=F32)


def wait_bytes(ref, sem):
    pltpu.make_async_copy(ref, ref, sem).wait()


def main_kernel(
    q_hbm, k_hbm, v_hbm, d_hbm, pack_hbm, docs_hbm,
    ret, retkv, place,
    q_in, k_in, v_in, d_in, pack, docs,
    send, recv, outb, kvsend, kv, kvout, dkv, pxs, pxr,
    scr, scr2, ks, vs, kts, vts, dks, dvs, bias,
    load_sem, in_send, in_recv, out_send, out_recv, doc_send, doc_recv,
    kvs_sem, kvr_sem, ks_sem, kr_sem, fws_sem, fwr_sem, pxs_sem, pxr_sem,
):
    my_dp = lax.axis_index("dp")
    my_ctx = lax.axis_index("ctx")
    z, y, x, core = my_dp // 4, my_dp % 4, my_ctx // 2, my_ctx % 2
    first = {Z: y, Y: z, X: z}
    second = {Z: x, Y: x, X: y}
    plane = {Z: z, Y: y, X: x}
    mine = {kind: first[kind] * 8 + second[kind] * 2 + core for kind in (Z, Y, X)}
    kinds = [u % 3 for u in range(UNITS)]

    def device(kind, index):
        a, b, c = index // 8, (index // 2) % 4, index % 2
        if kind == Z:
            return {"dp": z * 4 + a, "ctx": b * 2 + c}
        if kind == Y:
            return {"dp": a * 4 + y, "ctx": b * 2 + c}
        return {"dp": a * 4 + b, "ctx": x * 2 + c}

    def sequence(kind, index):
        a, b = index // 8, (index // 2) % 4
        return b * 4 + a if kind == Z else a * 4 + b

    def peer(kind, p):
        if kind == Z:
            return {"dp": p * 4 + y, "ctx": my_ctx}
        if kind == Y:
            return {"dp": z * 4 + p, "ctx": my_ctx}
        return {"dp": my_dp, "ctx": p * 2 + core}

    def remote(src, dst, send_sem, recv_sem, to):
        return pltpu.make_async_remote_copy(
            src_ref=src, dst_ref=dst, send_sem=send_sem, recv_sem=recv_sem, device_id=to, device_id_type=MESH
        )

    def loaders_of(ref, kind, p):
        every = slice(None)
        return ref.at[{Z: (p,), Y: (every, p), X: (every, every, p)}[kind]]

    def for_own(w, body):
        for c in range(2):
            u = c * OWN + w
            pl.when(core == c)(lambda u=u: body(u, kinds[u]))

    def to_chips(units, copy_to, own_copy):
        units = [(u, kinds[u]) for u in units]

        def step(i, carry):
            for u, kind in units:
                copy_to(u, kind, shifted(mine[kind] - core, 2 * ((i * STRIDE) & 15)) + u // OWN).start()
            return carry

        for u, kind in units:
            pl.when(core == u // OWN)(lambda u=u, kind=kind: own_copy(u, kind).start())
            pl.when(core != u // OWN)(lambda u=u, kind=kind: copy_to(u, kind, mine[kind] - core + u // OWN).start())
        lax.fori_loop(1, 16, step, 0)

    barrier = pltpu.get_barrier_semaphore()

    def greet(i, carry):
        for kind in (Z, Y, X):
            to = device(kind, shifted(mine[kind], (i * STRIDE) & 31))
            pl.semaphore_signal(barrier, inc=1, device_id=to, device_id_type=MESH)
        return carry

    lax.fori_loop(1, PLANE, greet, 0)

    load_kv = [
        pltpu.make_async_copy(src, dst, load_sem.at[i])
        for i, (src, dst) in enumerate(((pack_hbm, pack), (k_hbm, k_in), (v_hbm, v_in), (docs_hbm, docs.at[X])))
    ]
    for load in load_kv:
        load.start()
    part_wide = CHUNK_HEADS * HEAD_WIDTH
    for ch in range(CHUNKS):
        for u in range(UNITS):
            cols = pl.ds((u * CHUNKS + ch) * part_wide, part_wide)
            pltpu.make_async_copy(q_hbm.at[:, cols], q_in.at[:, cols], load_sem.at[4 + 2 * ch]).start()
            pltpu.make_async_copy(d_hbm.at[:, cols], d_in.at[:, cols], load_sem.at[5 + 2 * ch]).start()

    load_kv[0].wait()
    row = lax.broadcasted_iota(jnp.int32, (TOK_DEV, DEVICES), 0)
    by_row = jnp.where(row == pack[...], 1.0, 0.0).astype(F32)
    picks = jnp.transpose(by_row).astype(BF16)

    def pair_rows(a, b):
        a = a.reshape(SEQUENCES, BLOCKS, HEAD_WIDTH)
        b = b.reshape(SEQUENCES, BLOCKS, HEAD_WIDTH)
        return jnp.concatenate([a, b], axis=1).astype(BF16)

    load_kv[1].wait()
    load_kv[2].wait()
    for u in range(UNITS):
        cols = slice(u * HEAD_WIDTH, (u + 1) * HEAD_WIDTH)
        kvsend[u] = pair_rows(dot_nn(picks, k_in[:, cols]), dot_nn(picks, v_in[:, cols]))

    def pack_chunk(ch):
        wait_bytes(q_in.at[:, pl.ds(0, UNITS * part_wide)], load_sem.at[4 + 2 * ch])
        wait_bytes(d_in.at[:, pl.ds(0, UNITS * part_wide)], load_sem.at[5 + 2 * ch])
        for u in range(UNITS):
            for h in range(CHUNK_HEADS):
                head = (u * CHUNKS + ch) * CHUNK_HEADS + h
                cols = slice(head * HEAD_WIDTH, (head + 1) * HEAD_WIDTH)
                tile = pair_rows(dot_nn(picks, q_in[:, cols]), dot_nn(picks, d_in[:, cols]))
                send[ch, u, :, h * 16 : (h + 1) * 16] = tile

    pack_chunk(0)
    pl.semaphore_wait(barrier, 3 * (PLANE - 1))

    to_chips(
        range(UNITS),
        lambda u, kind, n: remote(
            kvsend.at[u, sequence(kind, n)], kv.at[u % OWN, plane[kind], mine[kind]],
            kvs_sem.at[u], kvr_sem.at[u % OWN], device(kind, n),
        ),
        lambda u, kind: pltpu.make_async_copy(
            kvsend.at[u, sequence(kind, mine[kind])], kv.at[u % OWN, plane[kind], mine[kind]], kvr_sem.at[u % OWN]
        ),
    )

    load_kv[3].wait()
    doc_to = {Z: {"dp": x * 4 + y, "ctx": z * 2 + core}, Y: {"dp": z * 4 + x, "ctx": y * 2 + core}}
    doc_stays = {Z: x == z, Y: x == y}
    for kind in (Z, Y):

        @pl.when(doc_stays[kind])
        def _():
            pltpu.make_async_copy(docs.at[X], docs.at[kind], doc_recv.at[kind]).start()

        @pl.when(jnp.logical_not(doc_stays[kind]))
        def _():
            remote(docs.at[X], docs.at[kind], doc_send.at[kind], doc_recv.at[kind], doc_to[kind]).start()

    def send_chunk(ch, w):
        to_chips(
            range(w, UNITS, OWN),
            lambda u, kind, n: remote(
                send.at[ch, u, sequence(kind, n)], recv.at[ch, u % OWN, mine[kind]],
                in_send.at[ch, u], in_recv.at[ch, u % OWN], device(kind, n),
            ),
            lambda u, kind: pltpu.make_async_copy(
                send.at[ch, u, sequence(kind, mine[kind])], recv.at[ch, u % OWN, mine[kind]], in_recv.at[ch, u % OWN]
            ),
        )

    def hand_on(u, kind):
        block = kv.at[u % OWN, plane[kind]]
        for d in range(1, 4):
            to = peer(kind, (plane[kind] + d) % 4)
            remote(block, block, fws_sem.at[u % OWN], fwr_sem.at[u % OWN], to).start()

    send_chunk(0, 0)
    pack_chunk(1)
    for w in range(OWN):
        wait_bytes(kv.at[w, 0], kvr_sem.at[w])
        for_own(w, hand_on)
    send_chunk(0, 1)
    send_chunk(1, 0)
    send_chunk(1, 1)

    goes = lax.broadcasted_iota(jnp.int32, (DEVICES, 2 * DEVICES), 0)
    lane = lax.broadcasted_iota(jnp.int32, (DEVICES, 2 * DEVICES), 1)
    same = goes == (lane >> 4) * BLOCKS + (lane & 7)
    upper = ((lane >> 3) & 1) == 1
    for t in range(2):
        spread = jnp.where(same & (upper == bool(t)), 1.0, 0.0).astype(BF16)
        place[t * TOK_DEV : (t + 1) * TOK_DEV] = dot_nn(by_row.astype(BF16), spread).astype(BF16)
    dks[...] = jnp.zeros_like(dks)
    dvs[...] = jnp.zeros_like(dvs)

    tile = (128, 128)
    lanes = lax.broadcasted_iota(jnp.int32, tile, 1)
    sub = lax.broadcasted_iota(jnp.int32, tile, 0)
    m = lanes >> 2
    loader = {Z: z * 32 + m, Y: (m >> 3) * 32 + y * 8 + (m & 7), X: (m >> 1) * 8 + x * 2 + (m & 1)}
    flat = scr.reshape(2 * SEQ, HEAD_WIDTH)
    for kind in (Y, Z):
        wait_bytes(docs.at[kind], doc_recv.at[kind])
    for w in range(OWN):
        query_at = jnp.where(core == 0, loader[kinds[w]], loader[kinds[OWN + w]])
        line = docs[jnp.where(core == 0, kinds[w], kinds[OWN + w])].astype(F32)
        parts = [line[:, k * 128 : (k + 1) * 128] for k in range(BLOCKS)]
        for k in range(BLOCKS):
            flat[k * 128 : (k + 1) * 128] = jnp.transpose(jnp.broadcast_to(parts[k], tile))
        select = jnp.where(sub == query_at, 1.0, 0.0).astype(BF16)
        query_docs = dot_nn(jnp.concatenate(parts, axis=0).astype(BF16), select)
        for i, (lo, hi) in enumerate(WINDOWS):
            for t in range(lo, hi, 128):
                for n in range(2):
                    k = 2 * i + n
                    live = (flat[t : t + 128] == query_docs[k : k + 1]) & (t + sub <= k * 128 + query_at)
                    at_row = BIAS_ROWS[i] + t - lo
                    bias[w, at_row : at_row + 128, n * 128 : (n + 1) * 128] = jnp.where(live, 0.0, -1e30)

    def keys_in_order(w):
        wait_bytes(kv.at[w, pl.ds(0, 3)], fwr_sem.at[w])

        def spread_kv(u, kind):
            for p in range(4):
                part = loaders_of(scr, kind, p)
                part[...] = kv[w, p].reshape(part.shape).astype(F32)

        for_own(w, spread_kv)
        for k in range(BLOCKS):
            rows = slice(k * 128, (k + 1) * 128)
            k_block = flat[pl.ds(k, 128, stride=16), :]
            v_block = flat[pl.ds(BLOCKS + k, 128, stride=16), :]
            ks[w, rows] = k_block.astype(BF16)
            vs[w, rows] = v_block.astype(BF16)
            kts[w, :, rows] = jnp.transpose(k_block).astype(BF16)
            vts[w, :, rows] = jnp.transpose(v_block).astype(BF16)

    def one_step(n, carry):
        ch, w = n // OWN, n % OWN
        for own in range(OWN):
            pl.when(n == own)(lambda own=own: keys_in_order(own))
        wait_bytes(recv.at[ch, w], in_recv.at[ch, w])
        flat[...] = recv[ch, w].reshape(2 * SEQ, HEAD_WIDTH).astype(F32)
        for i, (lo, hi) in enumerate(WINDOWS):

            def pair(start):
                parts = [flat[pl.ds(start + 2 * i + n, 128, stride=16), :] for n in range(2)]
                return jnp.concatenate(parts, axis=0)

            query = pair(0).astype(BF16)
            cotangent_f = pair(BLOCKS)
            cotangent = cotangent_f.astype(BF16)
            scores = dot_nt(ks[w, lo:hi], query) + bias[w, BIAS_ROWS[i] : BIAS_ROWS[i + 1]]
            best = jnp.max(scores, axis=0, keepdims=True)
            weights = jnp.exp2((scores - best) * (SCALE * math.log2(math.e)))
            total = jnp.sum(weights, axis=0, keepdims=True)
            probs = weights * (1.0 / total)
            probs_b = probs.astype(BF16)
            out_t = dot_nn(vts[w, :, lo:hi], probs_b)
            delta = jnp.sum(out_t.astype(BF16).astype(F32) * jnp.transpose(cotangent_f), axis=0, keepdims=True)
            dprob = dot_nt(vs[w, lo:hi], cotangent)
            dscore = (probs * (dprob - delta) * SCALE).astype(BF16)
            gq_t = dot_nn(kts[w, :, lo:hi], dscore)
            dks[w, lo:hi] += dot_nn(dscore, query)
            dvs[w, lo:hi] += dot_nn(probs_b, cotangent)
            out_rows, gq_rows = jnp.transpose(out_t), jnp.transpose(gq_t)
            for n in range(2):
                scr2[pl.ds(2 * i + n, 128, stride=16), :] = out_rows[n * 128 : (n + 1) * 128]
                scr2[pl.ds(BLOCKS + 2 * i + n, 128, stride=16), :] = gq_rows[n * 128 : (n + 1) * 128]
        outb[ch, w] = scr2[...].astype(BF16).reshape(PLANE, ROWS, HEAD_WIDTH)

        def exchange_gradients(u, kind):
            for p in range(4):
                dkv[w, p] = loaders_of(scr, kind, p)[...].reshape(PLANE, 16, HEAD_WIDTH)
            pxs[w] = dkv[w].astype(BF16)
            for d in range(1, 4):
                p = (plane[kind] + d) % 4
                remote(pxs.at[w, p], pxr.at[w, plane[kind]], pxs_sem.at[w], pxr_sem.at[w], peer(kind, p)).start()

        @pl.when(ch == CHUNKS - 1)
        def _():
            for k in range(BLOCKS):
                rows = slice(k * 128, (k + 1) * 128)
                flat[pl.ds(k, 128, stride=16), :] = dks[w, rows]
                flat[pl.ds(BLOCKS + k, 128, stride=16), :] = dvs[w, rows]
            for own in range(OWN):
                pl.when(w == own)(lambda own=own: for_own(own, exchange_gradients))

        def return_rows(u, kind):
            slot = ret.at[ch, u, sequence(kind, mine[kind])]

            def step(i, inner):
                to = shifted(mine[kind], (i * STRIDE) & 31)
                remote(outb.at[ch, w, to], slot, out_send.at[ch, w], out_recv.at[ch, u], device(kind, to)).start()
                return inner

            pltpu.make_async_copy(outb.at[ch, w, mine[kind]], slot, out_recv.at[ch, u]).start()
            lax.fori_loop(1, PLANE, step, 0)

        for own in range(OWN):
            pl.when(w == own)(lambda own=own: for_own(own, return_rows))
        return carry

    lax.fori_loop(0, CHUNKS * OWN, one_step, 0)

    def return_kv(u, kind):
        w = u % OWN
        total = dkv[w, plane[kind]]
        for d in range(1, 4):
            total = total + pxr[w, (plane[kind] + d) % 4].astype(F32)
        kvout[w] = total.astype(BF16)
        slot = retkv.at[u, sequence(kind, mine[kind])]

        def step(i, carry):
            to = shifted(mine[kind], (i * STRIDE) & 31)
            remote(kvout.at[w, to], slot, ks_sem.at[w], kr_sem.at[u], device(kind, to)).start()
            return carry

        pltpu.make_async_copy(kvout.at[w, mine[kind]], slot, kr_sem.at[u]).start()
        lax.fori_loop(1, PLANE, step, 0)

    for w in range(OWN):
        wait_bytes(pxr.at[w, pl.ds(0, 3)], pxr_sem.at[w])
        for_own(w, return_kv)

    for u in range(UNITS):
        for ch in range(CHUNKS):
            wait_bytes(ret.at[ch, u], out_recv.at[ch, u])
            wait_bytes(send.at[ch, u, pl.ds(0, 15)], in_send.at[ch, u])
        wait_bytes(retkv.at[u], kr_sem.at[u])
        wait_bytes(kvsend.at[u, pl.ds(0, 15)], kvs_sem.at[u])

        @pl.when(core != u // OWN)
        def _():
            for ch in range(CHUNKS):
                wait_bytes(send.at[ch, u, 0], in_send.at[ch, u])
            wait_bytes(kvsend.at[u, 0], kvs_sem.at[u])

    for w in range(OWN):
        for ch in range(CHUNKS):
            wait_bytes(outb.at[ch, w, pl.ds(0, PLANE - 1)], out_send.at[ch, w])
        wait_bytes(kv.at[w, pl.ds(0, 3)], fws_sem.at[w])
        wait_bytes(pxs.at[w, pl.ds(0, 3)], pxs_sem.at[w])
        wait_bytes(kvout.at[w, pl.ds(0, PLANE - 1)], ks_sem.at[w])
    for kind in (Z, Y):

        @pl.when(jnp.logical_not(doc_stays[kind]))
        def _():
            wait_bytes(docs.at[kind], doc_send.at[kind])


def unpack_kernel(ret, retkv, place, out, gq, gk, gv, out_s, gq_s, gk_s, gv_s, sems):
    copies = []

    def put(src, dst, cols):
        copies.append(pltpu.make_async_copy(src.at[:, cols], dst.at[:, cols], sems.at[len(copies)]))
        copies[-1].start()

    head = 0
    for u in range(UNITS):
        for ch in range(CHUNKS):
            for h in range(CHUNK_HEADS):
                rows = ret[ch, u, :, h * 16 : (h + 1) * 16].reshape(2 * DEVICES, HEAD_WIDTH)
                both = dot_nn(place[...], rows)
                cols = slice(head * HEAD_WIDTH, (head + 1) * HEAD_WIDTH)
                out_s[:, cols] = both[:TOK_DEV].astype(BF16)
                gq_s[:, cols] = both[TOK_DEV:]
                head += 1
            wide = CHUNK_HEADS * HEAD_WIDTH
            put(out_s, out, pl.ds((u * CHUNKS + ch) * wide, wide))
            put(gq_s, gq, pl.ds((u * CHUNKS + ch) * wide, wide))
    for u in range(UNITS):
        cols = slice(u * HEAD_WIDTH, (u + 1) * HEAD_WIDTH)
        both = dot_nn(place[...], retkv[u].reshape(2 * DEVICES, HEAD_WIDTH))
        gk_s[:, cols] = both[:TOK_DEV]
        gv_s[:, cols] = both[TOK_DEV:]
    put(gk_s, gk, pl.ds(0, KEY_HEADS * HEAD_WIDTH))
    put(gv_s, gv, pl.ds(0, KEY_HEADS * HEAD_WIDTH))
    for copy in copies:
        copy.wait()


def local(queries, loader_key_rows, loader_value_rows, output_gradient, packing, documents):
    out_rows = pltpu.VMEM((CHUNKS, UNITS, SEQUENCES, ROWS, HEAD_WIDTH), BF16)
    own_rows = pltpu.VMEM((CHUNKS, OWN, PLANE, ROWS, HEAD_WIDTH), BF16)
    seq = (OWN, SEQ, HEAD_WIDTH)
    turned = (OWN, HEAD_WIDTH, SEQ)
    kv_tiles = (UNITS, SEQUENCES, 16, HEAD_WIDTH)
    planes = (OWN, 4, PLANE, 16, HEAD_WIDTH)

    def copies(*shape):
        return pltpu.SemaphoreType.DMA(shape)

    operands = (queries, loader_key_rows, loader_value_rows, output_gradient, packing, documents)
    operands = [pltpu.with_memory_space_constraint(x, pltpu.HBM) for x in operands]
    ret, retkv, place = pl.pallas_call(
        main_kernel,
        out_shape=(
            jax.ShapeDtypeStruct(out_rows.shape, BF16),
            jax.ShapeDtypeStruct(kv_tiles, BF16),
            jax.ShapeDtypeStruct((2 * TOK_DEV, 2 * DEVICES), BF16),
        ),
        in_specs=[pl.BlockSpec(memory_space=pltpu.HBM)] * 6,
        out_specs=(pl.BlockSpec(memory_space=pltpu.VMEM),) * 3,
        scratch_shapes=[
            pltpu.VMEM(queries.shape, BF16),
            pltpu.VMEM(loader_key_rows.shape, BF16),
            pltpu.VMEM(loader_value_rows.shape, BF16),
            pltpu.VMEM(output_gradient.shape, BF16),
            pltpu.VMEM(packing.shape, jnp.int32),
            pltpu.VMEM((3, *documents.shape), jnp.int32),
            out_rows,
            own_rows,
            own_rows,
            pltpu.VMEM(kv_tiles, BF16),
            pltpu.VMEM(planes, BF16),
            pltpu.VMEM((OWN, PLANE, 16, HEAD_WIDTH), BF16),
            pltpu.VMEM(planes, F32),
            pltpu.VMEM(planes, BF16),
            pltpu.VMEM(planes, BF16),
            pltpu.VMEM((4, 4, 4, 2, 16, HEAD_WIDTH), F32),
            pltpu.VMEM((2 * SEQ, HEAD_WIDTH), F32),
            pltpu.VMEM(seq, BF16),
            pltpu.VMEM(seq, BF16),
            pltpu.VMEM(turned, BF16),
            pltpu.VMEM(turned, BF16),
            pltpu.VMEM(seq, F32),
            pltpu.VMEM(seq, F32),
            pltpu.VMEM((OWN, BIAS_ROWS[-1], QB), F32),
            copies(8),
            copies(CHUNKS, UNITS), copies(CHUNKS, OWN),
            copies(CHUNKS, OWN), copies(CHUNKS, UNITS),
            copies(2), copies(2),
            copies(UNITS), copies(OWN),
            copies(OWN), copies(UNITS),
            copies(OWN), copies(OWN),
            copies(OWN), copies(OWN),
        ],
        compiler_params=pltpu.CompilerParams(collective_id=0, has_side_effects=True, vmem_limit_bytes=48 << 20),
        name="exchange_attention",
    )(*operands)

    kv_shape = (TOK_DEV, KEY_HEADS * HEAD_WIDTH)
    shapes = ((queries.shape, BF16), (queries.shape, F32), (kv_shape, F32), (kv_shape, F32))
    return pl.pallas_call(
        unpack_kernel,
        out_shape=tuple(jax.ShapeDtypeStruct(*s) for s in shapes),
        in_specs=[pl.BlockSpec(memory_space=pltpu.VMEM)] * 3,
        out_specs=(pl.BlockSpec(memory_space=pltpu.HBM),) * 4,
        scratch_shapes=[pltpu.VMEM(*s) for s in shapes] + [pltpu.SemaphoreType.DMA((18,))],
        compiler_params=pltpu.CompilerParams(vmem_limit_bytes=32 << 20),
        name="rows_to_loader_order",
    )(ret, retkv, place)


def solution(mesh):
    rows = P(("dp", "ctx"), None)
    return jax.shard_map(
        local, mesh=mesh, in_specs=(rows,) * 5 + (P("dp", None),), out_specs=(rows,) * 4, check_vma=False
    )
```

```python
import math

import jax
import jax.numpy as jnp
from jax import lax
from jax.experimental import pallas as pl
from jax.experimental.pallas import tpu as pltpu
from jax.sharding import PartitionSpec as P

HEAD_WIDTH = 128
TOK_DEV = 128
N_CTX = 8
DEVICES = 128
SEQUENCES = 16
KEY_HEADS = 4
BLOCKS = 8
SEQ = 1024
QB = 256
DOC_MOST = 512
SCALE = 1.0 / math.sqrt(HEAD_WIDTH)
MESH = pl.DeviceIdType.MESH
F32 = jnp.float32
BF16 = jnp.bfloat16

Z, Y, X = range(3)
UNITS = KEY_HEADS
OWN = 2
CHUNKS = 2
CHUNK_HEADS = 4
PLANE = 32
ROWS = CHUNK_HEADS * 16
STRIDE = 13

WINDOWS = [(max(0, QB * i - DOC_MOST), QB * (i + 1)) for i in range(SEQ // QB)]
BIAS_ROWS = [sum(b - a for a, b in WINDOWS[:i]) for i in range(len(WINDOWS) + 1)]


def shifted(index, offset):
    low = 0b01010
    return (((index & low) + (offset & low)) ^ ((index ^ offset) & (31 - low))) & 31


def dot_nt(a, b):
    return lax.dot_general(a, b, (((1,), (1,)), ((), ())), preferred_element_type=F32)


def dot_nn(a, b):
    return jnp.dot(a, b, preferred_element_type=F32)


def wait_bytes(ref, sem):
    pltpu.make_async_copy(ref, ref, sem).wait()


def main_kernel(
    q_hbm, k_hbm, v_hbm, d_hbm, pack_hbm, docs_hbm,
    ret, retkv, place,
    q_in, k_in, v_in, d_in, pack, docs,
    send, recv, outb, kvsend, kv, kvout, dkv, pxs, pxr,
    scr, scr2, ks, vs, kts, vts, dks, dvs, bias,
    load_sem, in_send, in_recv, out_send, out_recv, doc_send, doc_recv,
    kvs_sem, kvr_sem, ks_sem, kr_sem, fws_sem, fwr_sem, pxs_sem, pxr_sem,
):
    my_dp = lax.axis_index("dp")
    my_ctx = lax.axis_index("ctx")
    z, y, x, core = my_dp // 4, my_dp % 4, my_ctx // 2, my_ctx % 2
    first = {Z: y, Y: z, X: z}
    second = {Z: x, Y: x, X: y}
    plane = {Z: z, Y: y, X: x}
    mine = {kind: first[kind] * 8 + second[kind] * 2 + core for kind in (Z, Y, X)}
    kinds = [u % 3 for u in range(UNITS)]

    def device(kind, index):
        a, b, c = index // 8, (index // 2) % 4, index % 2
        if kind == Z:
            return {"dp": z * 4 + a, "ctx": b * 2 + c}
        if kind == Y:
            return {"dp": a * 4 + y, "ctx": b * 2 + c}
        return {"dp": a * 4 + b, "ctx": x * 2 + c}

    def sequence(kind, index):
        a, b = index // 8, (index // 2) % 4
        return b * 4 + a if kind == Z else a * 4 + b

    def peer(kind, p):
        if kind == Z:
            return {"dp": p * 4 + y, "ctx": my_ctx}
        if kind == Y:
            return {"dp": z * 4 + p, "ctx": my_ctx}
        return {"dp": my_dp, "ctx": p * 2 + core}

    def remote(src, dst, send_sem, recv_sem, to):
        return pltpu.make_async_remote_copy(
            src_ref=src, dst_ref=dst, send_sem=send_sem, recv_sem=recv_sem, device_id=to, device_id_type=MESH
        )

    def loaders_of(ref, kind, p):
        every = slice(None)
        return ref.at[{Z: (p,), Y: (every, p), X: (every, every, p)}[kind]]

    def for_own(w, body):
        for c in range(2):
            u = c * OWN + w
            pl.when(core == c)(lambda u=u: body(u, kinds[u]))

    def to_chips(units, copy_to, own_copy):
        units = [(u, kinds[u]) for u in units]

        def step(i, carry):
            for u, kind in units:
                copy_to(u, kind, shifted(mine[kind] - core, 2 * ((i * STRIDE) & 15)) + u // OWN).start()
            return carry

        for u, kind in units:
            pl.when(core == u // OWN)(lambda u=u, kind=kind: own_copy(u, kind).start())
            pl.when(core != u // OWN)(lambda u=u, kind=kind: copy_to(u, kind, mine[kind] - core + u // OWN).start())
        lax.fori_loop(1, 16, step, 0)

    barrier = pltpu.get_barrier_semaphore()

    def greet(i, carry):
        for kind in (Z, Y, X):
            to = device(kind, shifted(mine[kind], (i * STRIDE) & 31))
            pl.semaphore_signal(barrier, inc=1, device_id=to, device_id_type=MESH)
        return carry

    lax.fori_loop(1, PLANE, greet, 0)

    load_kv = [
        pltpu.make_async_copy(src, dst, load_sem.at[i])
        for i, (src, dst) in enumerate(((pack_hbm, pack), (k_hbm, k_in), (v_hbm, v_in), (docs_hbm, docs.at[X])))
    ]
    for load in load_kv:
        load.start()
    part_wide = CHUNK_HEADS * HEAD_WIDTH
    for ch in range(CHUNKS):
        for u in range(UNITS):
            cols = pl.ds((u * CHUNKS + ch) * part_wide, part_wide)
            pltpu.make_async_copy(q_hbm.at[:, cols], q_in.at[:, cols], load_sem.at[4 + 2 * ch]).start()
            pltpu.make_async_copy(d_hbm.at[:, cols], d_in.at[:, cols], load_sem.at[5 + 2 * ch]).start()

    load_kv[0].wait()
    row = lax.broadcasted_iota(jnp.int32, (TOK_DEV, DEVICES), 0)
    by_row = jnp.where(row == pack[...], 1.0, 0.0).astype(F32)
    picks = jnp.transpose(by_row).astype(BF16)

    def pair_rows(a, b):
        a = a.reshape(SEQUENCES, BLOCKS, HEAD_WIDTH)
        b = b.reshape(SEQUENCES, BLOCKS, HEAD_WIDTH)
        return jnp.concatenate([a, b], axis=1).astype(BF16)

    load_kv[1].wait()
    load_kv[2].wait()
    k_rows, v_rows = dot_nn(picks, k_in[...]), dot_nn(picks, v_in[...])
    for u in range(UNITS):
        cols = slice(u * HEAD_WIDTH, (u + 1) * HEAD_WIDTH)
        kvsend[u] = pair_rows(k_rows[:, cols], v_rows[:, cols])

    def pack_chunk(ch):
        wait_bytes(q_in.at[:, pl.ds(0, UNITS * part_wide)], load_sem.at[4 + 2 * ch])
        wait_bytes(d_in.at[:, pl.ds(0, UNITS * part_wide)], load_sem.at[5 + 2 * ch])
        for u in range(UNITS):
            wide = slice((u * CHUNKS + ch) * part_wide, (u * CHUNKS + ch + 1) * part_wide)
            q_rows, d_rows = dot_nn(picks, q_in[:, wide]), dot_nn(picks, d_in[:, wide])
            for h in range(CHUNK_HEADS):
                cols = slice(h * HEAD_WIDTH, (h + 1) * HEAD_WIDTH)
                send[ch, u, :, h * 16 : (h + 1) * 16] = pair_rows(q_rows[:, cols], d_rows[:, cols])

    pack_chunk(0)
    pl.semaphore_wait(barrier, 3 * (PLANE - 1))

    to_chips(
        range(UNITS),
        lambda u, kind, n: remote(
            kvsend.at[u, sequence(kind, n)], kv.at[u % OWN, plane[kind], mine[kind]],
            kvs_sem.at[u], kvr_sem.at[u % OWN], device(kind, n),
        ),
        lambda u, kind: pltpu.make_async_copy(
            kvsend.at[u, sequence(kind, mine[kind])], kv.at[u % OWN, plane[kind], mine[kind]], kvr_sem.at[u % OWN]
        ),
    )

    load_kv[3].wait()
    doc_to = {Z: {"dp": x * 4 + y, "ctx": z * 2 + core}, Y: {"dp": z * 4 + x, "ctx": y * 2 + core}}
    doc_stays = {Z: x == z, Y: x == y}
    for kind in (Z, Y):

        @pl.when(doc_stays[kind])
        def _():
            pltpu.make_async_copy(docs.at[X], docs.at[kind], doc_recv.at[kind]).start()

        @pl.when(jnp.logical_not(doc_stays[kind]))
        def _():
            remote(docs.at[X], docs.at[kind], doc_send.at[kind], doc_recv.at[kind], doc_to[kind]).start()

    def send_chunk(ch, w):
        to_chips(
            range(w, UNITS, OWN),
            lambda u, kind, n: remote(
                send.at[ch, u, sequence(kind, n)], recv.at[ch, u % OWN, mine[kind]],
                in_send.at[ch, u], in_recv.at[ch, u % OWN], device(kind, n),
            ),
            lambda u, kind: pltpu.make_async_copy(
                send.at[ch, u, sequence(kind, mine[kind])], recv.at[ch, u % OWN, mine[kind]], in_recv.at[ch, u % OWN]
            ),
        )

    def hand_on(u, kind):
        block = kv.at[u % OWN, plane[kind]]
        for d in range(1, 4):
            to = peer(kind, (plane[kind] + d) % 4)
            remote(block, block, fws_sem.at[u % OWN], fwr_sem.at[u % OWN], to).start()

    send_chunk(0, 0)
    pack_chunk(1)
    for w in range(OWN):
        wait_bytes(kv.at[w, 0], kvr_sem.at[w])
        for_own(w, hand_on)
    send_chunk(0, 1)
    send_chunk(1, 0)
    send_chunk(1, 1)

    goes = lax.broadcasted_iota(jnp.int32, (DEVICES, 2 * DEVICES), 0)
    lane = lax.broadcasted_iota(jnp.int32, (DEVICES, 2 * DEVICES), 1)
    same = goes == (lane >> 4) * BLOCKS + (lane & 7)
    upper = ((lane >> 3) & 1) == 1
    for t in range(2):
        spread = jnp.where(same & (upper == bool(t)), 1.0, 0.0).astype(BF16)
        place[t * TOK_DEV : (t + 1) * TOK_DEV] = dot_nn(by_row.astype(BF16), spread).astype(BF16)
    dks[...] = jnp.zeros_like(dks)
    dvs[...] = jnp.zeros_like(dvs)

    tile = (128, 128)
    lanes = lax.broadcasted_iota(jnp.int32, tile, 1)
    sub = lax.broadcasted_iota(jnp.int32, tile, 0)
    m = lanes >> 2
    loader = {Z: z * 32 + m, Y: (m >> 3) * 32 + y * 8 + (m & 7), X: (m >> 1) * 8 + x * 2 + (m & 1)}
    flat = scr.reshape(2 * SEQ, HEAD_WIDTH)
    for kind in (Y, Z):
        wait_bytes(docs.at[kind], doc_recv.at[kind])
    for w in range(OWN):
        query_at = jnp.where(core == 0, loader[kinds[w]], loader[kinds[OWN + w]])
        line = docs[jnp.where(core == 0, kinds[w], kinds[OWN + w])].astype(F32)
        parts = [line[:, k * 128 : (k + 1) * 128] for k in range(BLOCKS)]
        for k in range(BLOCKS):
            flat[k * 128 : (k + 1) * 128] = jnp.transpose(jnp.broadcast_to(parts[k], tile))
        select = jnp.where(sub == query_at, 1.0, 0.0).astype(BF16)
        query_docs = dot_nn(jnp.concatenate(parts, axis=0).astype(BF16), select)
        for i, (lo, hi) in enumerate(WINDOWS):
            for t in range(lo, hi, 128):
                for n in range(2):
                    k = 2 * i + n
                    live = (flat[t : t + 128] == query_docs[k : k + 1]) & (t + sub <= k * 128 + query_at)
                    at_row = BIAS_ROWS[i] + t - lo
                    bias[w, at_row : at_row + 128, n * 128 : (n + 1) * 128] = jnp.where(live, 0.0, -1e30)

    def keys_in_order(w):
        wait_bytes(kv.at[w, pl.ds(0, 3)], fwr_sem.at[w])

        def spread_kv(u, kind):
            for p in range(4):
                part = loaders_of(scr, kind, p)
                part[...] = kv[w, p].reshape(part.shape).astype(F32)

        for_own(w, spread_kv)
        for k in range(BLOCKS):
            rows = slice(k * 128, (k + 1) * 128)
            k_block = flat[pl.ds(k, 128, stride=16), :]
            v_block = flat[pl.ds(BLOCKS + k, 128, stride=16), :]
            ks[w, rows] = k_block.astype(BF16)
            vs[w, rows] = v_block.astype(BF16)
            kts[w, :, rows] = jnp.transpose(k_block).astype(BF16)
            vts[w, :, rows] = jnp.transpose(v_block).astype(BF16)

    def one_step(n, carry):
        ch, w = n // OWN, n % OWN
        for own in range(OWN):
            pl.when(n == own)(lambda own=own: keys_in_order(own))
        wait_bytes(recv.at[ch, w], in_recv.at[ch, w])
        flat[...] = recv[ch, w].reshape(2 * SEQ, HEAD_WIDTH).astype(F32)
        for i, (lo, hi) in enumerate(WINDOWS):

            def pair(start):
                parts = [flat[pl.ds(start + 2 * i + n, 128, stride=16), :] for n in range(2)]
                return jnp.concatenate(parts, axis=0)

            query = pair(0).astype(BF16)
            cotangent_f = pair(BLOCKS)
            cotangent = cotangent_f.astype(BF16)
            scores = dot_nt(ks[w, lo:hi], query) + bias[w, BIAS_ROWS[i] : BIAS_ROWS[i + 1]]
            best = jnp.max(scores, axis=0, keepdims=True)
            weights = jnp.exp2((scores - best) * (SCALE * math.log2(math.e)))
            total = jnp.sum(weights, axis=0, keepdims=True)
            probs = weights * (1.0 / total)
            probs_b = probs.astype(BF16)
            out_t = dot_nn(vts[w, :, lo:hi], probs_b)
            delta = jnp.sum(out_t.astype(BF16).astype(F32) * jnp.transpose(cotangent_f), axis=0, keepdims=True)
            dprob = dot_nt(vs[w, lo:hi], cotangent)
            dscore = (probs * (dprob - delta) * SCALE).astype(BF16)
            gq_t = dot_nn(kts[w, :, lo:hi], dscore)
            dks[w, lo:hi] += dot_nn(dscore, query)
            dvs[w, lo:hi] += dot_nn(probs_b, cotangent)
            out_rows, gq_rows = jnp.transpose(out_t), jnp.transpose(gq_t)
            for n in range(2):
                scr2[pl.ds(2 * i + n, 128, stride=16), :] = out_rows[n * 128 : (n + 1) * 128]
                scr2[pl.ds(BLOCKS + 2 * i + n, 128, stride=16), :] = gq_rows[n * 128 : (n + 1) * 128]
        outb[ch, w] = scr2[...].astype(BF16).reshape(PLANE, ROWS, HEAD_WIDTH)

        def exchange_gradients(u, kind):
            for p in range(4):
                dkv[w, p] = loaders_of(scr, kind, p)[...].reshape(PLANE, 16, HEAD_WIDTH)
            pxs[w] = dkv[w].astype(BF16)
            for d in range(1, 4):
                p = (plane[kind] + d) % 4
                remote(pxs.at[w, p], pxr.at[w, plane[kind]], pxs_sem.at[w], pxr_sem.at[w], peer(kind, p)).start()

        @pl.when(ch == CHUNKS - 1)
        def _():
            for k in range(BLOCKS):
                rows = slice(k * 128, (k + 1) * 128)
                flat[pl.ds(k, 128, stride=16), :] = dks[w, rows]
                flat[pl.ds(BLOCKS + k, 128, stride=16), :] = dvs[w, rows]
            for own in range(OWN):
                pl.when(w == own)(lambda own=own: for_own(own, exchange_gradients))

        def return_rows(u, kind):
            slot = ret.at[ch, u, sequence(kind, mine[kind])]

            def step(i, inner):
                to = shifted(mine[kind], (i * STRIDE) & 31)
                remote(outb.at[ch, w, to], slot, out_send.at[ch, w], out_recv.at[ch, u], device(kind, to)).start()
                return inner

            pltpu.make_async_copy(outb.at[ch, w, mine[kind]], slot, out_recv.at[ch, u]).start()
            lax.fori_loop(1, PLANE, step, 0)

        for own in range(OWN):
            pl.when(w == own)(lambda own=own: for_own(own, return_rows))
        return carry

    lax.fori_loop(0, CHUNKS * OWN, one_step, 0)

    def return_kv(u, kind):
        w = u % OWN
        total = dkv[w, plane[kind]]
        for d in range(1, 4):
            total = total + pxr[w, (plane[kind] + d) % 4].astype(F32)
        kvout[w] = total.astype(BF16)
        slot = retkv.at[u, sequence(kind, mine[kind])]

        def step(i, carry):
            to = shifted(mine[kind], (i * STRIDE) & 31)
            remote(kvout.at[w, to], slot, ks_sem.at[w], kr_sem.at[u], device(kind, to)).start()
            return carry

        pltpu.make_async_copy(kvout.at[w, mine[kind]], slot, kr_sem.at[u]).start()
        lax.fori_loop(1, PLANE, step, 0)

    for w in range(OWN):
        wait_bytes(pxr.at[w, pl.ds(0, 3)], pxr_sem.at[w])
        for_own(w, return_kv)

    for u in range(UNITS):
        for ch in range(CHUNKS):
            wait_bytes(ret.at[ch, u], out_recv.at[ch, u])
            wait_bytes(send.at[ch, u, pl.ds(0, 15)], in_send.at[ch, u])
        wait_bytes(retkv.at[u], kr_sem.at[u])
        wait_bytes(kvsend.at[u, pl.ds(0, 15)], kvs_sem.at[u])

        @pl.when(core != u // OWN)
        def _():
            for ch in range(CHUNKS):
                wait_bytes(send.at[ch, u, 0], in_send.at[ch, u])
            wait_bytes(kvsend.at[u, 0], kvs_sem.at[u])

    for w in range(OWN):
        for ch in range(CHUNKS):
            wait_bytes(outb.at[ch, w, pl.ds(0, PLANE - 1)], out_send.at[ch, w])
        wait_bytes(kv.at[w, pl.ds(0, 3)], fws_sem.at[w])
        wait_bytes(pxs.at[w, pl.ds(0, 3)], pxs_sem.at[w])
        wait_bytes(kvout.at[w, pl.ds(0, PLANE - 1)], ks_sem.at[w])
    for kind in (Z, Y):

        @pl.when(jnp.logical_not(doc_stays[kind]))
        def _():
            wait_bytes(docs.at[kind], doc_send.at[kind])


def unpack_kernel(ret, retkv, place, out, gq, gk, gv, out_s, gq_s, gk_s, gv_s, sems):
    copies = []

    def put(src, dst, cols):
        copies.append(pltpu.make_async_copy(src.at[:, cols], dst.at[:, cols], sems.at[len(copies)]))
        copies[-1].start()

    head = 0
    for u in range(UNITS):
        for ch in range(CHUNKS):
            for h in range(0, CHUNK_HEADS, 2):
                rows = [ret[ch, u, :, n * 16 : (n + 1) * 16].reshape(2 * DEVICES, HEAD_WIDTH) for n in (h, h + 1)]
                both = dot_nn(place[...], jnp.concatenate(rows, axis=1))
                cols = slice(head * HEAD_WIDTH, (head + 2) * HEAD_WIDTH)
                out_s[:, cols] = both[:TOK_DEV].astype(BF16)
                gq_s[:, cols] = both[TOK_DEV:]
                head += 2
            wide = CHUNK_HEADS * HEAD_WIDTH
            put(out_s, out, pl.ds((u * CHUNKS + ch) * wide, wide))
            put(gq_s, gq, pl.ds((u * CHUNKS + ch) * wide, wide))
    for u in range(0, UNITS, 2):
        cols = slice(u * HEAD_WIDTH, (u + 2) * HEAD_WIDTH)
        rows = [retkv[n].reshape(2 * DEVICES, HEAD_WIDTH) for n in (u, u + 1)]
        both = dot_nn(place[...], jnp.concatenate(rows, axis=1))
        gk_s[:, cols] = both[:TOK_DEV]
        gv_s[:, cols] = both[TOK_DEV:]
    put(gk_s, gk, pl.ds(0, KEY_HEADS * HEAD_WIDTH))
    put(gv_s, gv, pl.ds(0, KEY_HEADS * HEAD_WIDTH))
    for copy in copies:
        copy.wait()


def local(queries, loader_key_rows, loader_value_rows, output_gradient, packing, documents):
    out_rows = pltpu.VMEM((CHUNKS, UNITS, SEQUENCES, ROWS, HEAD_WIDTH), BF16)
    own_rows = pltpu.VMEM((CHUNKS, OWN, PLANE, ROWS, HEAD_WIDTH), BF16)
    seq = (OWN, SEQ, HEAD_WIDTH)
    turned = (OWN, HEAD_WIDTH, SEQ)
    kv_tiles = (UNITS, SEQUENCES, 16, HEAD_WIDTH)
    planes = (OWN, 4, PLANE, 16, HEAD_WIDTH)

    def copies(*shape):
        return pltpu.SemaphoreType.DMA(shape)

    operands = (queries, loader_key_rows, loader_value_rows, output_gradient, packing, documents)
    operands = [pltpu.with_memory_space_constraint(x, pltpu.HBM) for x in operands]
    ret, retkv, place = pl.pallas_call(
        main_kernel,
        out_shape=(
            jax.ShapeDtypeStruct(out_rows.shape, BF16),
            jax.ShapeDtypeStruct(kv_tiles, BF16),
            jax.ShapeDtypeStruct((2 * TOK_DEV, 2 * DEVICES), BF16),
        ),
        in_specs=[pl.BlockSpec(memory_space=pltpu.HBM)] * 6,
        out_specs=(pl.BlockSpec(memory_space=pltpu.VMEM),) * 3,
        scratch_shapes=[
            pltpu.VMEM(queries.shape, BF16),
            pltpu.VMEM(loader_key_rows.shape, BF16),
            pltpu.VMEM(loader_value_rows.shape, BF16),
            pltpu.VMEM(output_gradient.shape, BF16),
            pltpu.VMEM(packing.shape, jnp.int32),
            pltpu.VMEM((3, *documents.shape), jnp.int32),
            out_rows,
            own_rows,
            own_rows,
            pltpu.VMEM(kv_tiles, BF16),
            pltpu.VMEM(planes, BF16),
            pltpu.VMEM((OWN, PLANE, 16, HEAD_WIDTH), BF16),
            pltpu.VMEM(planes, F32),
            pltpu.VMEM(planes, BF16),
            pltpu.VMEM(planes, BF16),
            pltpu.VMEM((4, 4, 4, 2, 16, HEAD_WIDTH), F32),
            pltpu.VMEM((2 * SEQ, HEAD_WIDTH), F32),
            pltpu.VMEM(seq, BF16),
            pltpu.VMEM(seq, BF16),
            pltpu.VMEM(turned, BF16),
            pltpu.VMEM(turned, BF16),
            pltpu.VMEM(seq, F32),
            pltpu.VMEM(seq, F32),
            pltpu.VMEM((OWN, BIAS_ROWS[-1], QB), F32),
            copies(8),
            copies(CHUNKS, UNITS), copies(CHUNKS, OWN),
            copies(CHUNKS, OWN), copies(CHUNKS, UNITS),
            copies(2), copies(2),
            copies(UNITS), copies(OWN),
            copies(OWN), copies(UNITS),
            copies(OWN), copies(OWN),
            copies(OWN), copies(OWN),
        ],
        compiler_params=pltpu.CompilerParams(collective_id=0, has_side_effects=True, vmem_limit_bytes=48 << 20),
        name="exchange_attention",
    )(*operands)

    kv_shape = (TOK_DEV, KEY_HEADS * HEAD_WIDTH)
    shapes = ((queries.shape, BF16), (queries.shape, F32), (kv_shape, F32), (kv_shape, F32))
    return pl.pallas_call(
        unpack_kernel,
        out_shape=tuple(jax.ShapeDtypeStruct(*s) for s in shapes),
        in_specs=[pl.BlockSpec(memory_space=pltpu.VMEM)] * 3,
        out_specs=(pl.BlockSpec(memory_space=pltpu.HBM),) * 4,
        scratch_shapes=[pltpu.VMEM(*s) for s in shapes] + [pltpu.SemaphoreType.DMA((18,))],
        compiler_params=pltpu.CompilerParams(vmem_limit_bytes=32 << 20),
        name="rows_to_loader_order",
    )(ret, retkv, place)


def solution(mesh):
    rows = P(("dp", "ctx"), None)
    return jax.shard_map(
        local, mesh=mesh, in_specs=(rows,) * 5 + (P("dp", None),), out_specs=(rows,) * 4, check_vma=False
    )
```

```python
import math

import jax
import jax.numpy as jnp
from jax import lax
from jax.experimental import pallas as pl
from jax.experimental.pallas import tpu as pltpu
from jax.sharding import PartitionSpec as P

HEAD_WIDTH = 128
TOK_DEV = 128
N_CTX = 8
DEVICES = 128
SEQUENCES = 16
KEY_HEADS = 4
BLOCKS = 8
SEQ = 1024
QB = 256
DOC_MOST = 512
SCALE = 1.0 / math.sqrt(HEAD_WIDTH)
MESH = pl.DeviceIdType.MESH
F32 = jnp.float32
BF16 = jnp.bfloat16

Z, Y, X = range(3)
UNITS = KEY_HEADS
OWN = 2
CHUNKS = 2
CHUNK_HEADS = 4
PLANE = 32
ROWS = CHUNK_HEADS * 16
STRIDE = 13

WINDOWS = [(max(0, QB * i - DOC_MOST), QB * (i + 1)) for i in range(SEQ // QB)]
BIAS_ROWS = [sum(b - a for a, b in WINDOWS[:i]) for i in range(len(WINDOWS) + 1)]


def shifted(index, offset):
    low = 0b01010
    return (((index & low) + (offset & low)) ^ ((index ^ offset) & (31 - low))) & 31


def dot_nt(a, b):
    return lax.dot_general(a, b, (((1,), (1,)), ((), ())), preferred_element_type=F32)


def dot_nn(a, b):
    return jnp.dot(a, b, preferred_element_type=F32)


def wait_bytes(ref, sem):
    pltpu.make_async_copy(ref, ref, sem).wait()


def main_kernel(
    q_hbm, k_hbm, v_hbm, d_hbm, pack_hbm, docs_hbm,
    ret, retkv, place,
    q_in, k_in, v_in, d_in, pack, docs,
    send, recv, outb, kvsend, kv, kvout, dkv, pxs, pxr,
    scr, scr2, ks, vs, kts, vts, dks, dvs, bias,
    load_sem, in_send, in_recv, out_send, out_recv, doc_send, doc_recv,
    kvs_sem, kvr_sem, ks_sem, kr_sem, fws_sem, fwr_sem, pxs_sem, pxr_sem,
):
    my_dp = lax.axis_index("dp")
    my_ctx = lax.axis_index("ctx")
    z, y, x, core = my_dp // 4, my_dp % 4, my_ctx // 2, my_ctx % 2
    first = {Z: y, Y: z, X: z}
    second = {Z: x, Y: x, X: y}
    plane = {Z: z, Y: y, X: x}
    mine = {kind: first[kind] * 8 + second[kind] * 2 + core for kind in (Z, Y, X)}
    kinds = [u % 3 for u in range(UNITS)]

    def device(kind, index):
        a, b, c = index // 8, (index // 2) % 4, index % 2
        if kind == Z:
            return {"dp": z * 4 + a, "ctx": b * 2 + c}
        if kind == Y:
            return {"dp": a * 4 + y, "ctx": b * 2 + c}
        return {"dp": a * 4 + b, "ctx": x * 2 + c}

    def sequence(kind, index):
        a, b = index // 8, (index // 2) % 4
        return b * 4 + a if kind == Z else a * 4 + b

    def peer(kind, p):
        if kind == Z:
            return {"dp": p * 4 + y, "ctx": my_ctx}
        if kind == Y:
            return {"dp": z * 4 + p, "ctx": my_ctx}
        return {"dp": my_dp, "ctx": p * 2 + core}

    def remote(src, dst, send_sem, recv_sem, to):
        return pltpu.make_async_remote_copy(
            src_ref=src, dst_ref=dst, send_sem=send_sem, recv_sem=recv_sem, device_id=to, device_id_type=MESH
        )

    def loaders_of(ref, kind, p):
        every = slice(None)
        return ref.at[{Z: (p,), Y: (every, p), X: (every, every, p)}[kind]]

    def for_own(w, body):
        for c in range(2):
            u = c * OWN + w
            pl.when(core == c)(lambda u=u: body(u, kinds[u]))

    def to_chips(units, copy_to, own_copy):
        units = [(u, kinds[u]) for u in units]

        def step(i, carry):
            for u, kind in units:
                copy_to(u, kind, shifted(mine[kind] - core, 2 * ((i * STRIDE) & 15)) + u // OWN).start()
            return carry

        for u, kind in units:
            pl.when(core == u // OWN)(lambda u=u, kind=kind: own_copy(u, kind).start())
            pl.when(core != u // OWN)(lambda u=u, kind=kind: copy_to(u, kind, mine[kind] - core + u // OWN).start())
        lax.fori_loop(1, 16, step, 0)

    barrier = pltpu.get_barrier_semaphore()

    def greet(i, carry):
        for kind in (Z, Y, X):
            to = device(kind, shifted(mine[kind], (i * STRIDE) & 31))
            pl.semaphore_signal(barrier, inc=1, device_id=to, device_id_type=MESH)
        return carry

    lax.fori_loop(1, PLANE, greet, 0)

    load_kv = [
        pltpu.make_async_copy(src, dst, load_sem.at[i])
        for i, (src, dst) in enumerate(((pack_hbm, pack), (k_hbm, k_in), (v_hbm, v_in), (docs_hbm, docs.at[X])))
    ]
    for load in load_kv:
        load.start()
    part_wide = CHUNK_HEADS * HEAD_WIDTH
    for ch in range(CHUNKS):
        for u in range(UNITS):
            cols = pl.ds((u * CHUNKS + ch) * part_wide, part_wide)
            pltpu.make_async_copy(q_hbm.at[:, cols], q_in.at[:, cols], load_sem.at[4 + 2 * ch]).start()
            pltpu.make_async_copy(d_hbm.at[:, cols], d_in.at[:, cols], load_sem.at[5 + 2 * ch]).start()

    load_kv[0].wait()
    row = lax.broadcasted_iota(jnp.int32, (TOK_DEV, DEVICES), 0)
    by_row = jnp.where(row == pack[...], 1.0, 0.0).astype(F32)
    picks = jnp.transpose(by_row).astype(BF16)

    def pair_rows(a, b):
        a = a.reshape(SEQUENCES, BLOCKS, HEAD_WIDTH)
        b = b.reshape(SEQUENCES, BLOCKS, HEAD_WIDTH)
        return jnp.concatenate([a, b], axis=1).astype(BF16)

    load_kv[1].wait()
    load_kv[2].wait()
    k_rows, v_rows = dot_nn(picks, k_in[...]), dot_nn(picks, v_in[...])
    for u in range(UNITS):
        cols = slice(u * HEAD_WIDTH, (u + 1) * HEAD_WIDTH)
        kvsend[u] = pair_rows(k_rows[:, cols], v_rows[:, cols])

    def pack_chunk(ch):
        wait_bytes(q_in.at[:, pl.ds(0, UNITS * part_wide)], load_sem.at[4 + 2 * ch])
        wait_bytes(d_in.at[:, pl.ds(0, UNITS * part_wide)], load_sem.at[5 + 2 * ch])
        for u in range(UNITS):
            wide = slice((u * CHUNKS + ch) * part_wide, (u * CHUNKS + ch + 1) * part_wide)
            q_rows, d_rows = dot_nn(picks, q_in[:, wide]), dot_nn(picks, d_in[:, wide])
            for h in range(CHUNK_HEADS):
                cols = slice(h * HEAD_WIDTH, (h + 1) * HEAD_WIDTH)
                send[ch, u, :, h * 16 : (h + 1) * 16] = pair_rows(q_rows[:, cols], d_rows[:, cols])

    pack_chunk(0)
    pl.semaphore_wait(barrier, 3 * (PLANE - 1))

    to_chips(
        range(UNITS),
        lambda u, kind, n: remote(
            kvsend.at[u, sequence(kind, n)], kv.at[u % OWN, plane[kind], mine[kind]],
            kvs_sem.at[u], kvr_sem.at[u % OWN], device(kind, n),
        ),
        lambda u, kind: pltpu.make_async_copy(
            kvsend.at[u, sequence(kind, mine[kind])], kv.at[u % OWN, plane[kind], mine[kind]], kvr_sem.at[u % OWN]
        ),
    )

    load_kv[3].wait()
    doc_to = {Z: {"dp": x * 4 + y, "ctx": z * 2 + core}, Y: {"dp": z * 4 + x, "ctx": y * 2 + core}}
    doc_stays = {Z: x == z, Y: x == y}
    for kind in (Z, Y):

        @pl.when(doc_stays[kind])
        def _():
            pltpu.make_async_copy(docs.at[X], docs.at[kind], doc_recv.at[kind]).start()

        @pl.when(jnp.logical_not(doc_stays[kind]))
        def _():
            remote(docs.at[X], docs.at[kind], doc_send.at[kind], doc_recv.at[kind], doc_to[kind]).start()

    def send_chunk(ch, w):
        to_chips(
            range(w, UNITS, OWN),
            lambda u, kind, n: remote(
                send.at[ch, u, sequence(kind, n)], recv.at[ch, u % OWN, mine[kind]],
                in_send.at[ch, u], in_recv.at[ch, u % OWN], device(kind, n),
            ),
            lambda u, kind: pltpu.make_async_copy(
                send.at[ch, u, sequence(kind, mine[kind])], recv.at[ch, u % OWN, mine[kind]], in_recv.at[ch, u % OWN]
            ),
        )

    def hand_on(u, kind):
        block = kv.at[u % OWN, plane[kind]]
        for d in range(1, 4):
            to = peer(kind, (plane[kind] + d) % 4)
            remote(block, block, fws_sem.at[u % OWN], fwr_sem.at[u % OWN], to).start()

    def drained(ch, w):
        for u in range(w, UNITS, OWN):
            wait_bytes(send.at[ch, u, pl.ds(0, 15)], in_send.at[ch, u])
            pl.when(core != u // OWN)(lambda u=u: wait_bytes(send.at[ch, u, 0], in_send.at[ch, u]))

    send_chunk(0, 0)
    pack_chunk(1)
    for w in range(OWN):
        wait_bytes(kv.at[w, 0], kvr_sem.at[w])
        for_own(w, hand_on)
    drained(0, 0)
    send_chunk(0, 1)

    goes = lax.broadcasted_iota(jnp.int32, (DEVICES, 2 * DEVICES), 0)
    lane = lax.broadcasted_iota(jnp.int32, (DEVICES, 2 * DEVICES), 1)
    same = goes == (lane >> 4) * BLOCKS + (lane & 7)
    upper = ((lane >> 3) & 1) == 1
    for t in range(2):
        spread = jnp.where(same & (upper == bool(t)), 1.0, 0.0).astype(BF16)
        place[t * TOK_DEV : (t + 1) * TOK_DEV] = dot_nn(by_row.astype(BF16), spread).astype(BF16)
    dks[...] = jnp.zeros_like(dks)
    dvs[...] = jnp.zeros_like(dvs)

    tile = (128, 128)
    lanes = lax.broadcasted_iota(jnp.int32, tile, 1)
    sub = lax.broadcasted_iota(jnp.int32, tile, 0)
    m = lanes >> 2
    loader = {Z: z * 32 + m, Y: (m >> 3) * 32 + y * 8 + (m & 7), X: (m >> 1) * 8 + x * 2 + (m & 1)}
    flat = scr.reshape(2 * SEQ, HEAD_WIDTH)
    for kind in (Y, Z):
        wait_bytes(docs.at[kind], doc_recv.at[kind])
    for w in range(OWN):
        query_at = jnp.where(core == 0, loader[kinds[w]], loader[kinds[OWN + w]])
        line = docs[jnp.where(core == 0, kinds[w], kinds[OWN + w])].astype(F32)
        parts = [line[:, k * 128 : (k + 1) * 128] for k in range(BLOCKS)]
        for k in range(BLOCKS):
            flat[k * 128 : (k + 1) * 128] = jnp.transpose(jnp.broadcast_to(parts[k], tile))
        select = jnp.where(sub == query_at, 1.0, 0.0).astype(BF16)
        query_docs = dot_nn(jnp.concatenate(parts, axis=0).astype(BF16), select)
        for i, (lo, hi) in enumerate(WINDOWS):
            for t in range(lo, hi, 128):
                for n in range(2):
                    k = 2 * i + n
                    live = (flat[t : t + 128] == query_docs[k : k + 1]) & (t + sub <= k * 128 + query_at)
                    at_row = BIAS_ROWS[i] + t - lo
                    bias[w, at_row : at_row + 128, n * 128 : (n + 1) * 128] = jnp.where(live, 0.0, -1e30)

    def keys_in_order(w):
        wait_bytes(kv.at[w, pl.ds(0, 3)], fwr_sem.at[w])

        def spread_kv(u, kind):
            for p in range(4):
                part = loaders_of(scr, kind, p)
                part[...] = kv[w, p].reshape(part.shape).astype(F32)

        for_own(w, spread_kv)
        for k in range(BLOCKS):
            rows = slice(k * 128, (k + 1) * 128)
            k_block = flat[pl.ds(k, 128, stride=16), :]
            v_block = flat[pl.ds(BLOCKS + k, 128, stride=16), :]
            ks[w, rows] = k_block.astype(BF16)
            vs[w, rows] = v_block.astype(BF16)
            kts[w, :, rows] = jnp.transpose(k_block).astype(BF16)
            vts[w, :, rows] = jnp.transpose(v_block).astype(BF16)

    def one_step(n, carry):
        ch, w = n // OWN, n % OWN
        for own in range(OWN):
            pl.when(n == own)(lambda own=own: keys_in_order(own))
        wait_bytes(recv.at[ch, w], in_recv.at[ch, w])
        flat[...] = recv[ch, w].reshape(2 * SEQ, HEAD_WIDTH).astype(F32)
        for i, (lo, hi) in enumerate(WINDOWS):

            def pair(start):
                parts = [flat[pl.ds(start + 2 * i + n, 128, stride=16), :] for n in range(2)]
                return jnp.concatenate(parts, axis=0)

            query = pair(0).astype(BF16)
            cotangent_f = pair(BLOCKS)
            cotangent = cotangent_f.astype(BF16)
            scores = dot_nt(ks[w, lo:hi], query) + bias[w, BIAS_ROWS[i] : BIAS_ROWS[i + 1]]
            best = jnp.max(scores, axis=0, keepdims=True)
            weights = jnp.exp2((scores - best) * (SCALE * math.log2(math.e)))
            total = jnp.sum(weights, axis=0, keepdims=True)
            probs = weights * (1.0 / total)
            probs_b = probs.astype(BF16)
            out_t = dot_nn(vts[w, :, lo:hi], probs_b)
            delta = jnp.sum(out_t.astype(BF16).astype(F32) * jnp.transpose(cotangent_f), axis=0, keepdims=True)
            dprob = dot_nt(vs[w, lo:hi], cotangent)
            dscore = (probs * (dprob - delta) * SCALE).astype(BF16)
            gq_t = dot_nn(kts[w, :, lo:hi], dscore)
            dks[w, lo:hi] += dot_nn(dscore, query)
            dvs[w, lo:hi] += dot_nn(probs_b, cotangent)
            out_rows, gq_rows = jnp.transpose(out_t), jnp.transpose(gq_t)
            for n in range(2):
                scr2[pl.ds(2 * i + n, 128, stride=16), :] = out_rows[n * 128 : (n + 1) * 128]
                scr2[pl.ds(BLOCKS + 2 * i + n, 128, stride=16), :] = gq_rows[n * 128 : (n + 1) * 128]
        outb[ch, w] = scr2[...].astype(BF16).reshape(PLANE, ROWS, HEAD_WIDTH)

        def exchange_gradients(u, kind):
            for p in range(4):
                dkv[w, p] = loaders_of(scr, kind, p)[...].reshape(PLANE, 16, HEAD_WIDTH)
            pxs[w] = dkv[w].astype(BF16)
            for d in range(1, 4):
                p = (plane[kind] + d) % 4
                remote(pxs.at[w, p], pxr.at[w, plane[kind]], pxs_sem.at[w], pxr_sem.at[w], peer(kind, p)).start()

        @pl.when(ch == CHUNKS - 1)
        def _():
            for k in range(BLOCKS):
                rows = slice(k * 128, (k + 1) * 128)
                flat[pl.ds(k, 128, stride=16), :] = dks[w, rows]
                flat[pl.ds(BLOCKS + k, 128, stride=16), :] = dvs[w, rows]
            for own in range(OWN):
                pl.when(w == own)(lambda own=own: for_own(own, exchange_gradients))

        def return_rows(u, kind):
            slot = ret.at[ch, u, sequence(kind, mine[kind])]

            def step(i, inner):
                to = shifted(mine[kind], (i * STRIDE) & 31)
                remote(outb.at[ch, w, to], slot, out_send.at[ch, w], out_recv.at[ch, u], device(kind, to)).start()
                return inner

            pltpu.make_async_copy(outb.at[ch, w, mine[kind]], slot, out_recv.at[ch, u]).start()
            lax.fori_loop(1, PLANE, step, 0)

        for own in range(OWN):
            pl.when(w == own)(lambda own=own: for_own(own, return_rows))
        return carry

    drained(0, 1)
    send_chunk(1, 0)
    send_chunk(1, 1)
    lax.fori_loop(0, CHUNKS * OWN, one_step, 0)

    def return_kv(u, kind):
        w = u % OWN
        total = dkv[w, plane[kind]]
        for d in range(1, 4):
            total = total + pxr[w, (plane[kind] + d) % 4].astype(F32)
        kvout[w] = total.astype(BF16)
        slot = retkv.at[u, sequence(kind, mine[kind])]

        def step(i, carry):
            to = shifted(mine[kind], (i * STRIDE) & 31)
            remote(kvout.at[w, to], slot, ks_sem.at[w], kr_sem.at[u], device(kind, to)).start()
            return carry

        pltpu.make_async_copy(kvout.at[w, mine[kind]], slot, kr_sem.at[u]).start()
        lax.fori_loop(1, PLANE, step, 0)

    for w in range(OWN):
        wait_bytes(pxr.at[w, pl.ds(0, 3)], pxr_sem.at[w])
        for_own(w, return_kv)

    for u in range(UNITS):
        for ch in range(CHUNKS):
            wait_bytes(ret.at[ch, u], out_recv.at[ch, u])
        wait_bytes(retkv.at[u], kr_sem.at[u])
        wait_bytes(kvsend.at[u, pl.ds(0, 15)], kvs_sem.at[u])

        @pl.when(core != u // OWN)
        def _():
            wait_bytes(kvsend.at[u, 0], kvs_sem.at[u])

    for w in range(OWN):
        for ch in range(CHUNKS):
            wait_bytes(outb.at[ch, w, pl.ds(0, PLANE - 1)], out_send.at[ch, w])
        wait_bytes(kv.at[w, pl.ds(0, 3)], fws_sem.at[w])
        wait_bytes(pxs.at[w, pl.ds(0, 3)], pxs_sem.at[w])
        wait_bytes(kvout.at[w, pl.ds(0, PLANE - 1)], ks_sem.at[w])
    drained(1, 0)
    drained(1, 1)
    for kind in (Z, Y):

        @pl.when(jnp.logical_not(doc_stays[kind]))
        def _():
            wait_bytes(docs.at[kind], doc_send.at[kind])


def unpack_kernel(ret, retkv, place, out, gq, gk, gv, out_s, gq_s, gk_s, gv_s, sems):
    copies = []

    def put(src, dst, cols):
        copies.append(pltpu.make_async_copy(src.at[:, cols], dst.at[:, cols], sems.at[len(copies)]))
        copies[-1].start()

    head = 0
    for u in range(UNITS):
        for ch in range(CHUNKS):
            for h in range(0, CHUNK_HEADS, 2):
                rows = [ret[ch, u, :, n * 16 : (n + 1) * 16].reshape(2 * DEVICES, HEAD_WIDTH) for n in (h, h + 1)]
                both = dot_nn(place[...], jnp.concatenate(rows, axis=1))
                cols = slice(head * HEAD_WIDTH, (head + 2) * HEAD_WIDTH)
                out_s[:, cols] = both[:TOK_DEV].astype(BF16)
                gq_s[:, cols] = both[TOK_DEV:]
                head += 2
            wide = CHUNK_HEADS * HEAD_WIDTH
            put(out_s, out, pl.ds((u * CHUNKS + ch) * wide, wide))
            put(gq_s, gq, pl.ds((u * CHUNKS + ch) * wide, wide))
    for u in range(0, UNITS, 2):
        cols = slice(u * HEAD_WIDTH, (u + 2) * HEAD_WIDTH)
        rows = [retkv[n].reshape(2 * DEVICES, HEAD_WIDTH) for n in (u, u + 1)]
        both = dot_nn(place[...], jnp.concatenate(rows, axis=1))
        gk_s[:, cols] = both[:TOK_DEV]
        gv_s[:, cols] = both[TOK_DEV:]
    put(gk_s, gk, pl.ds(0, KEY_HEADS * HEAD_WIDTH))
    put(gv_s, gv, pl.ds(0, KEY_HEADS * HEAD_WIDTH))
    for copy in copies:
        copy.wait()


def local(queries, loader_key_rows, loader_value_rows, output_gradient, packing, documents):
    out_rows = pltpu.VMEM((CHUNKS, UNITS, SEQUENCES, ROWS, HEAD_WIDTH), BF16)
    own_rows = pltpu.VMEM((CHUNKS, OWN, PLANE, ROWS, HEAD_WIDTH), BF16)
    seq = (OWN, SEQ, HEAD_WIDTH)
    turned = (OWN, HEAD_WIDTH, SEQ)
    kv_tiles = (UNITS, SEQUENCES, 16, HEAD_WIDTH)
    planes = (OWN, 4, PLANE, 16, HEAD_WIDTH)

    def copies(*shape):
        return pltpu.SemaphoreType.DMA(shape)

    operands = (queries, loader_key_rows, loader_value_rows, output_gradient, packing, documents)
    operands = [pltpu.with_memory_space_constraint(x, pltpu.HBM) for x in operands]
    ret, retkv, place = pl.pallas_call(
        main_kernel,
        out_shape=(
            jax.ShapeDtypeStruct(out_rows.shape, BF16),
            jax.ShapeDtypeStruct(kv_tiles, BF16),
            jax.ShapeDtypeStruct((2 * TOK_DEV, 2 * DEVICES), BF16),
        ),
        in_specs=[pl.BlockSpec(memory_space=pltpu.HBM)] * 6,
        out_specs=(pl.BlockSpec(memory_space=pltpu.VMEM),) * 3,
        scratch_shapes=[
            pltpu.VMEM(queries.shape, BF16),
            pltpu.VMEM(loader_key_rows.shape, BF16),
            pltpu.VMEM(loader_value_rows.shape, BF16),
            pltpu.VMEM(output_gradient.shape, BF16),
            pltpu.VMEM(packing.shape, jnp.int32),
            pltpu.VMEM((3, *documents.shape), jnp.int32),
            out_rows,
            own_rows,
            own_rows,
            pltpu.VMEM(kv_tiles, BF16),
            pltpu.VMEM(planes, BF16),
            pltpu.VMEM((OWN, PLANE, 16, HEAD_WIDTH), BF16),
            pltpu.VMEM(planes, F32),
            pltpu.VMEM(planes, BF16),
            pltpu.VMEM(planes, BF16),
            pltpu.VMEM((4, 4, 4, 2, 16, HEAD_WIDTH), F32),
            pltpu.VMEM((2 * SEQ, HEAD_WIDTH), F32),
            pltpu.VMEM(seq, BF16),
            pltpu.VMEM(seq, BF16),
            pltpu.VMEM(turned, BF16),
            pltpu.VMEM(turned, BF16),
            pltpu.VMEM(seq, F32),
            pltpu.VMEM(seq, F32),
            pltpu.VMEM((OWN, BIAS_ROWS[-1], QB), F32),
            copies(8),
            copies(CHUNKS, UNITS), copies(CHUNKS, OWN),
            copies(CHUNKS, OWN), copies(CHUNKS, UNITS),
            copies(2), copies(2),
            copies(UNITS), copies(OWN),
            copies(OWN), copies(UNITS),
            copies(OWN), copies(OWN),
            copies(OWN), copies(OWN),
        ],
        compiler_params=pltpu.CompilerParams(collective_id=0, has_side_effects=True, vmem_limit_bytes=48 << 20),
        name="exchange_attention",
    )(*operands)

    kv_shape = (TOK_DEV, KEY_HEADS * HEAD_WIDTH)
    shapes = ((queries.shape, BF16), (queries.shape, F32), (kv_shape, F32), (kv_shape, F32))
    return pl.pallas_call(
        unpack_kernel,
        out_shape=tuple(jax.ShapeDtypeStruct(*s) for s in shapes),
        in_specs=[pl.BlockSpec(memory_space=pltpu.VMEM)] * 3,
        out_specs=(pl.BlockSpec(memory_space=pltpu.HBM),) * 4,
        scratch_shapes=[pltpu.VMEM(*s) for s in shapes] + [pltpu.SemaphoreType.DMA((18,))],
        compiler_params=pltpu.CompilerParams(vmem_limit_bytes=32 << 20),
        name="rows_to_loader_order",
    )(ret, retkv, place)


def solution(mesh):
    rows = P(("dp", "ctx"), None)
    return jax.shard_map(
        local, mesh=mesh, in_specs=(rows,) * 5 + (P("dp", None),), out_specs=(rows,) * 4, check_vma=False
    )
```

```python
import math

import jax
import jax.numpy as jnp
from jax import lax
from jax.experimental import pallas as pl
from jax.experimental.pallas import tpu as pltpu
from jax.sharding import PartitionSpec as P

HEAD_WIDTH = 128
TOK_DEV = 128
N_CTX = 8
DEVICES = 128
SEQUENCES = 16
KEY_HEADS = 4
BLOCKS = 8
SEQ = 1024
QB = 256
DOC_MOST = 512
SCALE = 1.0 / math.sqrt(HEAD_WIDTH)
MESH = pl.DeviceIdType.MESH
F32 = jnp.float32
BF16 = jnp.bfloat16

Z, Y, X = range(3)
UNITS = KEY_HEADS
OWN = 2
CHUNKS = 2
CHUNK_HEADS = 4
PLANE = 32
ROWS = CHUNK_HEADS * 16
STRIDE = 13

WINDOWS = [(max(0, QB * i - DOC_MOST), QB * (i + 1)) for i in range(SEQ // QB)]
BIAS_ROWS = [sum(b - a for a, b in WINDOWS[:i]) for i in range(len(WINDOWS) + 1)]


def shifted(index, offset):
    low = 0b01010
    return (((index & low) + (offset & low)) ^ ((index ^ offset) & (31 - low))) & 31


def dot_nt(a, b):
    return lax.dot_general(a, b, (((1,), (1,)), ((), ())), preferred_element_type=F32)


def dot_nn(a, b):
    return jnp.dot(a, b, preferred_element_type=F32)


def wait_bytes(ref, sem):
    pltpu.make_async_copy(ref, ref, sem).wait()


def main_kernel(
    q_hbm, k_hbm, v_hbm, d_hbm, pack_hbm, docs_hbm,
    ret, retkv, place,
    q_in, k_in, v_in, d_in, pack, docs,
    send, recv, outb, kvsend, kv, kvout, dkv, pxs, pxr,
    scr, scr2, ks, vs, kts, vts, dks, dvs, bias,
    load_sem, in_send, in_recv, out_send, out_recv, doc_send, doc_recv,
    kvs_sem, kvr_sem, ks_sem, kr_sem, fws_sem, fwr_sem, pxs_sem, pxr_sem,
):
    my_dp = lax.axis_index("dp")
    my_ctx = lax.axis_index("ctx")
    z, y, x, core = my_dp // 4, my_dp % 4, my_ctx // 2, my_ctx % 2
    first = {Z: y, Y: z, X: z}
    second = {Z: x, Y: x, X: y}
    plane = {Z: z, Y: y, X: x}
    mine = {kind: first[kind] * 8 + second[kind] * 2 + core for kind in (Z, Y, X)}
    kinds = [u % 3 for u in range(UNITS)]

    def device(kind, index):
        a, b, c = index // 8, (index // 2) % 4, index % 2
        if kind == Z:
            return {"dp": z * 4 + a, "ctx": b * 2 + c}
        if kind == Y:
            return {"dp": a * 4 + y, "ctx": b * 2 + c}
        return {"dp": a * 4 + b, "ctx": x * 2 + c}

    def sequence(kind, index):
        a, b = index // 8, (index // 2) % 4
        return b * 4 + a if kind == Z else a * 4 + b

    def peer(kind, p):
        if kind == Z:
            return {"dp": p * 4 + y, "ctx": my_ctx}
        if kind == Y:
            return {"dp": z * 4 + p, "ctx": my_ctx}
        return {"dp": my_dp, "ctx": p * 2 + core}

    def remote(src, dst, send_sem, recv_sem, to):
        return pltpu.make_async_remote_copy(
            src_ref=src, dst_ref=dst, send_sem=send_sem, recv_sem=recv_sem, device_id=to, device_id_type=MESH
        )

    def loaders_of(ref, kind, p):
        every = slice(None)
        return ref.at[{Z: (p,), Y: (every, p), X: (every, every, p)}[kind]]

    def for_own(w, body):
        for c in range(2):
            u = c * OWN + w
            pl.when(core == c)(lambda u=u: body(u, kinds[u]))

    def to_chips(units, copy_to, own_copy):
        units = [(u, kinds[u]) for u in units]

        def step(i, carry):
            for u, kind in units:
                copy_to(u, kind, shifted(mine[kind] - core, 2 * ((i * STRIDE) & 15)) + u // OWN).start()
            return carry

        for u, kind in units:
            pl.when(core == u // OWN)(lambda u=u, kind=kind: own_copy(u, kind).start())
            pl.when(core != u // OWN)(lambda u=u, kind=kind: copy_to(u, kind, mine[kind] - core + u // OWN).start())
        lax.fori_loop(1, 16, step, 0)

    barrier = pltpu.get_barrier_semaphore()

    def greet(i, carry):
        for kind in (Z, Y, X):
            to = device(kind, shifted(mine[kind], (i * STRIDE) & 31))
            pl.semaphore_signal(barrier, inc=1, device_id=to, device_id_type=MESH)
        return carry

    lax.fori_loop(1, PLANE, greet, 0)

    load_kv = [
        pltpu.make_async_copy(src, dst, load_sem.at[i])
        for i, (src, dst) in enumerate(((pack_hbm, pack), (k_hbm, k_in), (v_hbm, v_in), (docs_hbm, docs.at[X])))
    ]
    for load in load_kv:
        load.start()
    part_wide = CHUNK_HEADS * HEAD_WIDTH
    for ch in range(CHUNKS):
        for u in range(UNITS):
            cols = pl.ds((u * CHUNKS + ch) * part_wide, part_wide)
            pltpu.make_async_copy(q_hbm.at[:, cols], q_in.at[:, cols], load_sem.at[4 + 2 * ch]).start()
            pltpu.make_async_copy(d_hbm.at[:, cols], d_in.at[:, cols], load_sem.at[5 + 2 * ch]).start()

    load_kv[0].wait()
    row = lax.broadcasted_iota(jnp.int32, (TOK_DEV, DEVICES), 0)
    by_row = jnp.where(row == pack[...], 1.0, 0.0).astype(F32)
    picks = jnp.transpose(by_row).astype(BF16)

    def pair_rows(a, b):
        a = a.reshape(SEQUENCES, BLOCKS, HEAD_WIDTH)
        b = b.reshape(SEQUENCES, BLOCKS, HEAD_WIDTH)
        return jnp.concatenate([a, b], axis=1).astype(BF16)

    load_kv[1].wait()
    load_kv[2].wait()
    k_rows, v_rows = dot_nn(picks, k_in[...]), dot_nn(picks, v_in[...])
    for u in range(UNITS):
        cols = slice(u * HEAD_WIDTH, (u + 1) * HEAD_WIDTH)
        kvsend[u] = pair_rows(k_rows[:, cols], v_rows[:, cols])

    def pack_chunk(ch):
        wait_bytes(q_in.at[:, pl.ds(0, UNITS * part_wide)], load_sem.at[4 + 2 * ch])
        wait_bytes(d_in.at[:, pl.ds(0, UNITS * part_wide)], load_sem.at[5 + 2 * ch])
        for u in range(UNITS):
            wide = slice((u * CHUNKS + ch) * part_wide, (u * CHUNKS + ch + 1) * part_wide)
            q_rows, d_rows = dot_nn(picks, q_in[:, wide]), dot_nn(picks, d_in[:, wide])
            for h in range(CHUNK_HEADS):
                cols = slice(h * HEAD_WIDTH, (h + 1) * HEAD_WIDTH)
                send[ch, u, :, h * 16 : (h + 1) * 16] = pair_rows(q_rows[:, cols], d_rows[:, cols])

    pack_chunk(0)
    pl.semaphore_wait(barrier, 3 * (PLANE - 1))

    to_chips(
        range(UNITS),
        lambda u, kind, n: remote(
            kvsend.at[u, sequence(kind, n)], kv.at[u % OWN, plane[kind], mine[kind]],
            kvs_sem.at[u], kvr_sem.at[u % OWN], device(kind, n),
        ),
        lambda u, kind: pltpu.make_async_copy(
            kvsend.at[u, sequence(kind, mine[kind])], kv.at[u % OWN, plane[kind], mine[kind]], kvr_sem.at[u % OWN]
        ),
    )

    load_kv[3].wait()
    doc_to = {Z: {"dp": x * 4 + y, "ctx": z * 2 + core}, Y: {"dp": z * 4 + x, "ctx": y * 2 + core}}
    doc_stays = {Z: x == z, Y: x == y}
    for kind in (Z, Y):

        @pl.when(doc_stays[kind])
        def _():
            pltpu.make_async_copy(docs.at[X], docs.at[kind], doc_recv.at[kind]).start()

        @pl.when(jnp.logical_not(doc_stays[kind]))
        def _():
            remote(docs.at[X], docs.at[kind], doc_send.at[kind], doc_recv.at[kind], doc_to[kind]).start()

    def send_chunk(ch, w):
        to_chips(
            range(w, UNITS, OWN),
            lambda u, kind, n: remote(
                send.at[ch, u, sequence(kind, n)], recv.at[ch, u % OWN, mine[kind]],
                in_send.at[ch, u], in_recv.at[ch, u % OWN], device(kind, n),
            ),
            lambda u, kind: pltpu.make_async_copy(
                send.at[ch, u, sequence(kind, mine[kind])], recv.at[ch, u % OWN, mine[kind]], in_recv.at[ch, u % OWN]
            ),
        )

    def hand_on(u, kind):
        block = kv.at[u % OWN, plane[kind]]
        for d in range(1, 4):
            to = peer(kind, (plane[kind] + d) % 4)
            remote(block, block, fws_sem.at[u % OWN], fwr_sem.at[u % OWN], to).start()

    def drained(ch, w):
        for u in range(w, UNITS, OWN):
            wait_bytes(send.at[ch, u, pl.ds(0, 15)], in_send.at[ch, u])
            pl.when(core != u // OWN)(lambda u=u: wait_bytes(send.at[ch, u, 0], in_send.at[ch, u]))

    send_chunk(0, 0)
    pack_chunk(1)
    for w in range(OWN):
        wait_bytes(kv.at[w, 0], kvr_sem.at[w])
        for_own(w, hand_on)
    send_chunk(0, 1)

    goes = lax.broadcasted_iota(jnp.int32, (DEVICES, 2 * DEVICES), 0)
    lane = lax.broadcasted_iota(jnp.int32, (DEVICES, 2 * DEVICES), 1)
    same = goes == (lane >> 4) * BLOCKS + (lane & 7)
    upper = ((lane >> 3) & 1) == 1
    for t in range(2):
        spread = jnp.where(same & (upper == bool(t)), 1.0, 0.0).astype(BF16)
        place[t * TOK_DEV : (t + 1) * TOK_DEV] = dot_nn(by_row.astype(BF16), spread).astype(BF16)
    dks[...] = jnp.zeros_like(dks)
    dvs[...] = jnp.zeros_like(dvs)

    tile = (128, 128)
    lanes = lax.broadcasted_iota(jnp.int32, tile, 1)
    sub = lax.broadcasted_iota(jnp.int32, tile, 0)
    m = lanes >> 2
    loader = {Z: z * 32 + m, Y: (m >> 3) * 32 + y * 8 + (m & 7), X: (m >> 1) * 8 + x * 2 + (m & 1)}
    flat = scr.reshape(2 * SEQ, HEAD_WIDTH)
    for kind in (Y, Z):
        wait_bytes(docs.at[kind], doc_recv.at[kind])
    for w in range(OWN):
        query_at = jnp.where(core == 0, loader[kinds[w]], loader[kinds[OWN + w]])
        line = docs[jnp.where(core == 0, kinds[w], kinds[OWN + w])].astype(F32)
        parts = [line[:, k * 128 : (k + 1) * 128] for k in range(BLOCKS)]
        for k in range(BLOCKS):
            flat[k * 128 : (k + 1) * 128] = jnp.transpose(jnp.broadcast_to(parts[k], tile))
        select = jnp.where(sub == query_at, 1.0, 0.0).astype(BF16)
        query_docs = dot_nn(jnp.concatenate(parts, axis=0).astype(BF16), select)
        for i, (lo, hi) in enumerate(WINDOWS):
            for t in range(lo, hi, 128):
                for n in range(2):
                    k = 2 * i + n
                    live = (flat[t : t + 128] == query_docs[k : k + 1]) & (t + sub <= k * 128 + query_at)
                    at_row = BIAS_ROWS[i] + t - lo
                    bias[w, at_row : at_row + 128, n * 128 : (n + 1) * 128] = jnp.where(live, 0.0, -1e30)

    def keys_in_order(w):
        wait_bytes(kv.at[w, pl.ds(0, 3)], fwr_sem.at[w])

        def spread_kv(u, kind):
            for p in range(4):
                part = loaders_of(scr, kind, p)
                part[...] = kv[w, p].reshape(part.shape).astype(F32)

        for_own(w, spread_kv)
        for k in range(BLOCKS):
            rows = slice(k * 128, (k + 1) * 128)
            k_block = flat[pl.ds(k, 128, stride=16), :]
            v_block = flat[pl.ds(BLOCKS + k, 128, stride=16), :]
            ks[w, rows] = k_block.astype(BF16)
            vs[w, rows] = v_block.astype(BF16)
            kts[w, :, rows] = jnp.transpose(k_block).astype(BF16)
            vts[w, :, rows] = jnp.transpose(v_block).astype(BF16)

    def one_step(n, carry):
        ch, w = n // OWN, n % OWN
        for own in range(OWN):
            pl.when(n == own)(lambda own=own: keys_in_order(own))
        wait_bytes(recv.at[ch, w], in_recv.at[ch, w])
        flat[...] = recv[ch, w].reshape(2 * SEQ, HEAD_WIDTH).astype(F32)
        for i, (lo, hi) in enumerate(WINDOWS):

            def pair(start):
                parts = [flat[pl.ds(start + 2 * i + n, 128, stride=16), :] for n in range(2)]
                return jnp.concatenate(parts, axis=0)

            query = pair(0).astype(BF16)
            cotangent_f = pair(BLOCKS)
            cotangent = cotangent_f.astype(BF16)
            scores = dot_nt(ks[w, lo:hi], query) + bias[w, BIAS_ROWS[i] : BIAS_ROWS[i + 1]]
            best = jnp.max(scores, axis=0, keepdims=True)
            weights = jnp.exp2((scores - best) * (SCALE * math.log2(math.e)))
            total = jnp.sum(weights, axis=0, keepdims=True)
            probs = weights * (1.0 / total)
            probs_b = probs.astype(BF16)
            out_t = dot_nn(vts[w, :, lo:hi], probs_b)
            delta = jnp.sum(out_t.astype(BF16).astype(F32) * jnp.transpose(cotangent_f), axis=0, keepdims=True)
            dprob = dot_nt(vs[w, lo:hi], cotangent)
            dscore = (probs * (dprob - delta) * SCALE).astype(BF16)
            gq_t = dot_nn(kts[w, :, lo:hi], dscore)
            dks[w, lo:hi] += dot_nn(dscore, query)
            dvs[w, lo:hi] += dot_nn(probs_b, cotangent)
            out_rows, gq_rows = jnp.transpose(out_t), jnp.transpose(gq_t)
            for n in range(2):
                scr2[pl.ds(2 * i + n, 128, stride=16), :] = out_rows[n * 128 : (n + 1) * 128]
                scr2[pl.ds(BLOCKS + 2 * i + n, 128, stride=16), :] = gq_rows[n * 128 : (n + 1) * 128]
        outb[ch, w] = scr2[...].astype(BF16).reshape(PLANE, ROWS, HEAD_WIDTH)

        def exchange_gradients(u, kind):
            for p in range(4):
                dkv[w, p] = loaders_of(scr, kind, p)[...].reshape(PLANE, 16, HEAD_WIDTH)
            pxs[w] = dkv[w].astype(BF16)
            for d in range(1, 4):
                p = (plane[kind] + d) % 4
                remote(pxs.at[w, p], pxr.at[w, plane[kind]], pxs_sem.at[w], pxr_sem.at[w], peer(kind, p)).start()

        @pl.when(ch == CHUNKS - 1)
        def _():
            for k in range(BLOCKS):
                rows = slice(k * 128, (k + 1) * 128)
                flat[pl.ds(k, 128, stride=16), :] = dks[w, rows]
                flat[pl.ds(BLOCKS + k, 128, stride=16), :] = dvs[w, rows]
            for own in range(OWN):
                pl.when(w == own)(lambda own=own: for_own(own, exchange_gradients))

        def return_rows(u, kind):
            slot = ret.at[ch, u, sequence(kind, mine[kind])]

            def step(i, inner):
                to = shifted(mine[kind], (i * STRIDE) & 31)
                remote(outb.at[ch, w, to], slot, out_send.at[ch, w], out_recv.at[ch, u], device(kind, to)).start()
                return inner

            pltpu.make_async_copy(outb.at[ch, w, mine[kind]], slot, out_recv.at[ch, u]).start()
            lax.fori_loop(1, PLANE, step, 0)

        for own in range(OWN):
            pl.when(w == own)(lambda own=own: for_own(own, return_rows))
        return carry

    drained(0, 0)
    send_chunk(1, 0)
    send_chunk(1, 1)
    lax.fori_loop(0, CHUNKS * OWN, one_step, 0)

    def return_kv(u, kind):
        w = u % OWN
        total = dkv[w, plane[kind]]
        for d in range(1, 4):
            total = total + pxr[w, (plane[kind] + d) % 4].astype(F32)
        kvout[w] = total.astype(BF16)
        slot = retkv.at[u, sequence(kind, mine[kind])]

        def step(i, carry):
            to = shifted(mine[kind], (i * STRIDE) & 31)
            remote(kvout.at[w, to], slot, ks_sem.at[w], kr_sem.at[u], device(kind, to)).start()
            return carry

        pltpu.make_async_copy(kvout.at[w, mine[kind]], slot, kr_sem.at[u]).start()
        lax.fori_loop(1, PLANE, step, 0)

    for w in range(OWN):
        wait_bytes(pxr.at[w, pl.ds(0, 3)], pxr_sem.at[w])
        for_own(w, return_kv)

    for u in range(UNITS):
        for ch in range(CHUNKS):
            wait_bytes(ret.at[ch, u], out_recv.at[ch, u])
        wait_bytes(retkv.at[u], kr_sem.at[u])
        wait_bytes(kvsend.at[u, pl.ds(0, 15)], kvs_sem.at[u])

        @pl.when(core != u // OWN)
        def _():
            wait_bytes(kvsend.at[u, 0], kvs_sem.at[u])

    for w in range(OWN):
        for ch in range(CHUNKS):
            wait_bytes(outb.at[ch, w, pl.ds(0, PLANE - 1)], out_send.at[ch, w])
        wait_bytes(kv.at[w, pl.ds(0, 3)], fws_sem.at[w])
        wait_bytes(pxs.at[w, pl.ds(0, 3)], pxs_sem.at[w])
        wait_bytes(kvout.at[w, pl.ds(0, PLANE - 1)], ks_sem.at[w])
    drained(0, 1)
    drained(1, 0)
    drained(1, 1)
    for kind in (Z, Y):

        @pl.when(jnp.logical_not(doc_stays[kind]))
        def _():
            wait_bytes(docs.at[kind], doc_send.at[kind])


def unpack_kernel(ret, retkv, place, out, gq, gk, gv, out_s, gq_s, gk_s, gv_s, sems):
    copies = []

    def put(src, dst, cols):
        copies.append(pltpu.make_async_copy(src.at[:, cols], dst.at[:, cols], sems.at[len(copies)]))
        copies[-1].start()

    head = 0
    for u in range(UNITS):
        for ch in range(CHUNKS):
            for h in range(0, CHUNK_HEADS, 2):
                rows = [ret[ch, u, :, n * 16 : (n + 1) * 16].reshape(2 * DEVICES, HEAD_WIDTH) for n in (h, h + 1)]
                both = dot_nn(place[...], jnp.concatenate(rows, axis=1))
                cols = slice(head * HEAD_WIDTH, (head + 2) * HEAD_WIDTH)
                out_s[:, cols] = both[:TOK_DEV].astype(BF16)
                gq_s[:, cols] = both[TOK_DEV:]
                head += 2
            wide = CHUNK_HEADS * HEAD_WIDTH
            put(out_s, out, pl.ds((u * CHUNKS + ch) * wide, wide))
            put(gq_s, gq, pl.ds((u * CHUNKS + ch) * wide, wide))
    for u in range(0, UNITS, 2):
        cols = slice(u * HEAD_WIDTH, (u + 2) * HEAD_WIDTH)
        rows = [retkv[n].reshape(2 * DEVICES, HEAD_WIDTH) for n in (u, u + 1)]
        both = dot_nn(place[...], jnp.concatenate(rows, axis=1))
        gk_s[:, cols] = both[:TOK_DEV]
        gv_s[:, cols] = both[TOK_DEV:]
    put(gk_s, gk, pl.ds(0, KEY_HEADS * HEAD_WIDTH))
    put(gv_s, gv, pl.ds(0, KEY_HEADS * HEAD_WIDTH))
    for copy in copies:
        copy.wait()


def local(queries, loader_key_rows, loader_value_rows, output_gradient, packing, documents):
    out_rows = pltpu.VMEM((CHUNKS, UNITS, SEQUENCES, ROWS, HEAD_WIDTH), BF16)
    own_rows = pltpu.VMEM((CHUNKS, OWN, PLANE, ROWS, HEAD_WIDTH), BF16)
    seq = (OWN, SEQ, HEAD_WIDTH)
    turned = (OWN, HEAD_WIDTH, SEQ)
    kv_tiles = (UNITS, SEQUENCES, 16, HEAD_WIDTH)
    planes = (OWN, 4, PLANE, 16, HEAD_WIDTH)

    def copies(*shape):
        return pltpu.SemaphoreType.DMA(shape)

    operands = (queries, loader_key_rows, loader_value_rows, output_gradient, packing, documents)
    operands = [pltpu.with_memory_space_constraint(x, pltpu.HBM) for x in operands]
    ret, retkv, place = pl.pallas_call(
        main_kernel,
        out_shape=(
            jax.ShapeDtypeStruct(out_rows.shape, BF16),
            jax.ShapeDtypeStruct(kv_tiles, BF16),
            jax.ShapeDtypeStruct((2 * TOK_DEV, 2 * DEVICES), BF16),
        ),
        in_specs=[pl.BlockSpec(memory_space=pltpu.HBM)] * 6,
        out_specs=(pl.BlockSpec(memory_space=pltpu.VMEM),) * 3,
        scratch_shapes=[
            pltpu.VMEM(queries.shape, BF16),
            pltpu.VMEM(loader_key_rows.shape, BF16),
            pltpu.VMEM(loader_value_rows.shape, BF16),
            pltpu.VMEM(output_gradient.shape, BF16),
            pltpu.VMEM(packing.shape, jnp.int32),
            pltpu.VMEM((3, *documents.shape), jnp.int32),
            out_rows,
            own_rows,
            own_rows,
            pltpu.VMEM(kv_tiles, BF16),
            pltpu.VMEM(planes, BF16),
            pltpu.VMEM((OWN, PLANE, 16, HEAD_WIDTH), BF16),
            pltpu.VMEM(planes, F32),
            pltpu.VMEM(planes, BF16),
            pltpu.VMEM(planes, BF16),
            pltpu.VMEM((4, 4, 4, 2, 16, HEAD_WIDTH), F32),
            pltpu.VMEM((2 * SEQ, HEAD_WIDTH), F32),
            pltpu.VMEM(seq, BF16),
            pltpu.VMEM(seq, BF16),
            pltpu.VMEM(turned, BF16),
            pltpu.VMEM(turned, BF16),
            pltpu.VMEM(seq, F32),
            pltpu.VMEM(seq, F32),
            pltpu.VMEM((OWN, BIAS_ROWS[-1], QB), F32),
            copies(8),
            copies(CHUNKS, UNITS), copies(CHUNKS, OWN),
            copies(CHUNKS, OWN), copies(CHUNKS, UNITS),
            copies(2), copies(2),
            copies(UNITS), copies(OWN),
            copies(OWN), copies(UNITS),
            copies(OWN), copies(OWN),
            copies(OWN), copies(OWN),
        ],
        compiler_params=pltpu.CompilerParams(collective_id=0, has_side_effects=True, vmem_limit_bytes=48 << 20),
        name="exchange_attention",
    )(*operands)

    kv_shape = (TOK_DEV, KEY_HEADS * HEAD_WIDTH)
    shapes = ((queries.shape, BF16), (queries.shape, F32), (kv_shape, F32), (kv_shape, F32))
    return pl.pallas_call(
        unpack_kernel,
        out_shape=tuple(jax.ShapeDtypeStruct(*s) for s in shapes),
        in_specs=[pl.BlockSpec(memory_space=pltpu.VMEM)] * 3,
        out_specs=(pl.BlockSpec(memory_space=pltpu.HBM),) * 4,
        scratch_shapes=[pltpu.VMEM(*s) for s in shapes] + [pltpu.SemaphoreType.DMA((18,))],
        compiler_params=pltpu.CompilerParams(vmem_limit_bytes=32 << 20),
        name="rows_to_loader_order",
    )(ret, retkv, place)


def solution(mesh):
    rows = P(("dp", "ctx"), None)
    return jax.shard_map(
        local, mesh=mesh, in_specs=(rows,) * 5 + (P("dp", None),), out_specs=(rows,) * 4, check_vma=False
    )
```
